32 devices in a mesh: grp: 2 (over y), slab: 4 (over z), mem: 2 (over x), sub: 2 (over core).
Axes of the slice: x: 2, y: 2, z: 4, core: 2. Of those that a mesh axis runs over, the one named last changes fastest.
Arguments:
- state: bfloat16 [256, 32768], P('mem', ('grp', 'slab', 'sub')), parts along dimension 1, may hold values from -6 to 6
- centers: int32 [512], P('grp'), parts along dimension 0, may hold values from 0 to 16383, as said below
- half_width: int32 [512], P('grp'), parts along dimension 0, may hold values from 4 to 71
- radius: int32 [512], P('grp'), parts along dimension 0, may hold values from 2048 to 8192
- order: int32 [512], P('grp'), parts along dimension 0, may hold values from 0 to 255, each once
- obs_var: float32 [512], P('grp'), parts along dimension 0, may hold values from 0.1 to 1
Outputs:
- analysis: bfloat16 [256, 32768], P('mem', ('grp', 'slab', 'sub')), parts along dimension 1
The draws below stay inside these ranges and needn't reach their ends.
There are 2 independent parts, one for each index of `grp`. The reference program is written for one: setup_inputs(seed, part) draws one part's arguments, and reference() takes and returns one part's arrays. A program takes and returns all parts, laid end to end along the dimension named above; each array names one. Nothing has to cross between parts.
Inputs may be any that keep to these rules, and one draw needn't show every extreme that they name: order holds every observation number once. Observations 4 k to 4 k + 3 have centers within 6 rows of a common site row, which the first of them sits on; centers are clipped to the grid.
All inputs are finite; a program needn't handle non-finite values.
Results may differ from the reference program's by a relative error of at most 0.0049.
Values may be sent and summed in bfloat16 or wider, within the bound.
A program may use at most 64 MiB of HBM per device.

```python
import math
import jax
import jax.numpy as jnp
from jax import lax

M = 256
P_SIZE = 128
BATCHES = 2
ROWS_DEV = 2048
NROWS = 16384
NOBS = 256


def draw_centers(key, part):
    site_key = jax.random.fold_in(key, 11)
    jitter_key = jax.random.fold_in(key, 12)
    site_count = NOBS // 4
    site_rows = jax.random.randint(site_key, (site_count,), 0, NROWS)
    slot_index = lax.iota(jnp.int32, site_count)
    site_rows = jnp.where(slot_index == 0, 0, jnp.where(slot_index == 1, NROWS - 1, site_rows))
    spread = ROWS_DEV // 512 + 2
    jitter = jax.random.randint(jitter_key, (NOBS,), -spread, spread + 1)
    obs_index = lax.iota(jnp.int32, NOBS)
    jitter = jnp.where(obs_index % 4 == 0, 0, jitter)
    centers = jnp.repeat(site_rows, 4) + jitter
    return jnp.clip(centers, 0, NROWS - 1).astype(jnp.int32)


def place_ends(result, stream_key, smallest, high):
    longest = result.shape.index(max(result.shape))
    spots = []
    for shift in (0, 1):
        where = [jax.random.randint(jax.random.fold_in(stream_key, axis), (), 0, length) for axis, length in enumerate(result.shape)]
        where[longest] = (where[longest] + shift) % result.shape[longest]
        spots.append(tuple(where))
    return result.at[spots[0]].set(smallest).at[spots[1]].set(high)


def block_scale(key, shape, shards, least, high):
    def one(position, shards_of):
        heights = jax.random.uniform(jax.random.fold_in(jax.random.fold_in(key, 6), position), (shards_of,), jnp.float32, least / len(shards), high / len(shards))
        return jnp.repeat(jnp.exp(heights), shape[position] // shards_of).reshape((-1,) + (1,) * (len(shape) - position - 1))

    gain = one(*shards[0])
    for cut in shards[1:]:
        gain = gain * one(*cut)
    return gain


def gaussian(key, dims, deviation, reach, split=(), kind=jnp.bfloat16):
    drawn = deviation * jax.random.normal(key, dims, jnp.float32)
    if split:
        drawn = drawn * block_scale(key, dims, split, -0.22, 0.18)
    return jnp.clip(drawn, -reach, reach).astype(kind)


def setup_inputs(seed: int = 0, part: int = 0) -> dict:
    keys = jax.random.split(jax.random.key(seed), 7)
    own_keys = jax.random.split(jax.random.fold_in(keys[6], part), 7)
    state = gaussian(own_keys[0], (M, NROWS), 1.0, 6.0, ((0, 2), (1, 8)))
    centers = draw_centers(jax.random.fold_in(jax.random.fold_in(keys[6], part), 71), part)
    half_width = place_ends(jax.random.randint(own_keys[2], (NOBS,), 4, ROWS_DEV // 32 + 8), jax.random.fold_in(own_keys[2], 1), 4, (ROWS_DEV // 32 + 8) - 1).astype(jnp.int32)
    radius = place_ends(jax.random.randint(own_keys[3], (NOBS,), ROWS_DEV, 4 * ROWS_DEV + 1), jax.random.fold_in(own_keys[3], 1), ROWS_DEV, 4 * ROWS_DEV).astype(jnp.int32)
    order = jax.random.permutation(own_keys[4], NOBS).astype(jnp.int32)
    obs_var = jnp.clip(jnp.exp(jax.random.uniform(own_keys[5], (NOBS,), jnp.float32, math.log(0.1), math.log(1.0))), 0.1, 1.0)
    return {"state": state, "centers": centers, "half_width": half_width, "radius": radius, "order": order, "obs_var": obs_var}


floor_level = math.exp(-2.0)

def geometry(first_row, row_count, center_rows, half_rows, radius_rows):
    rows_all = first_row + lax.iota(jnp.int32, row_count)
    distance = (rows_all[None, :] - center_rows[:, None]).astype(jnp.float32)
    half_f = half_rows.astype(jnp.float32)[:, None]
    footprint = (jnp.maximum(jnp.exp(-2.0 * distance * distance / (half_f * half_f)) - floor_level, 0.0) / jnp.sqrt(half_f)).astype(jnp.bfloat16)
    taper_rows = jnp.square(jnp.maximum(1.0 - jnp.abs(distance) / radius_rows.astype(jnp.float32)[:, None], 0.0))
    return (footprint, taper_rows)

def gain_terms(projected, variance):
    high = lax.Precision.HIGHEST
    covariance = jnp.dot(projected.T.astype(jnp.float32), projected.astype(jnp.float32), precision=high, preferred_element_type=jnp.float32) / (M - 1) + jnp.diag(variance)
    factor = jnp.linalg.cholesky(covariance)
    identity = jnp.eye(P_SIZE, dtype=jnp.float32)
    inner_inv = lax.linalg.triangular_solve(factor + jnp.diag(jnp.sqrt(variance)), identity, left_side=True, lower=True)
    gain_mat = lax.linalg.triangular_solve(factor, inner_inv, left_side=True, lower=True, transpose_a=True)
    weights = jnp.dot(projected.astype(jnp.float32), gain_mat.T.astype(jnp.float32), precision=high, preferred_element_type=jnp.float32).astype(jnp.bfloat16)
    return (weights, projected.astype(jnp.bfloat16))

def reference(state, centers, half_width, radius, order, obs_var):
    high = lax.Precision.HIGHEST
    ensemble = state
    for batch in range(BATCHES):
        picked = order[batch * P_SIZE:(batch + 1) * P_SIZE]
        footprint, taper_rows = geometry(0, NROWS, centers[picked], half_width[picked], radius[picked])
        ens_f = ensemble.astype(jnp.float32)
        projected = jnp.dot(ens_f.astype(jnp.float32), footprint.astype(jnp.float32).T.astype(jnp.float32), precision=high, preferred_element_type=jnp.float32)
        weights, projected_b = gain_terms(projected, obs_var[picked])
        cross_cov = jnp.dot(projected_b.astype(jnp.float32).T.astype(jnp.float32), ens_f.astype(jnp.float32), precision=high, preferred_element_type=jnp.float32)
        tapered = (taper_rows * cross_cov / (M - 1)).astype(jnp.bfloat16)
        ensemble = (ens_f - jnp.dot(weights.astype(jnp.float32), tapered.astype(jnp.float32), precision=high, preferred_element_type=jnp.float32)).astype(jnp.bfloat16)
    return ensemble
```

```python
import functools
import math

import jax
import jax.numpy as jnp
from jax import lax
from jax.experimental import pallas as pl
from jax.experimental.pallas import tpu as pltpu
from jax.sharding import PartitionSpec as P

M = 256
P_SIZE = 128
BATCHES = 2
BLOCK = 16
SPLIT = 4

FLOOR = math.exp(-2.0)
F32 = jnp.float32
BF16 = jnp.bfloat16
HIGH = lax.Precision.HIGHEST
LAST = (((1,), (1,)), ((), ()))
FIRST = (((0,), (0,)), ((), ()))


def each(start, stop, body):
    if stop - start <= 16:
        for i in range(start, stop):
            body(i)
    else:

        def step(i, carry):
            body(i)
            return carry

        lax.fori_loop(start, stop, step, 0)


def split3(x):
    high = x.astype(BF16)
    rest = x - high.astype(F32)
    mid = rest.astype(BF16)
    low = (rest - mid.astype(F32)).astype(BF16)
    return high, mid, low


def sweep(work, inv, solved, root, first=0, last=P_SIZE // BLOCK, beside=None):
    b = BLOCK
    width = work.shape[1] // P_SIZE

    def step(k, carry):
        r0 = pl.multiple_of(k * b, b)
        parts = [work[pl.ds(r0, b), g * P_SIZE : (g + 1) * P_SIZE] for g in range(width)]
        roots = root[pl.ds(r0, b), :]
        rolled = pltpu.roll(parts[0], lax.rem(P_SIZE - r0, P_SIZE), 1)
        cols = [jnp.broadcast_to(rolled[:, j : j + 1], (b, P_SIZE)) for j in range(b)]
        row_id = lax.broadcasted_iota(jnp.int32, (b, P_SIZE), 0)
        for j in range(b):
            pivot = cols[j][j : j + 1, :]
            scale = lax.rsqrt(pivot)
            scale_m = 1.0 / (pivot * scale + roots[j : j + 1, :])
            column = jnp.where(row_id > j, cols[j] * scale, 0.0)
            for i in range(j + 1, b):
                cols[i] = cols[i] - column * column[i : i + 1, :]
            for g in range(width):
                row = parts[g][j : j + 1, :] * (scale if g < 2 else scale_m)
                parts[g] = jnp.where(row_id == j, row, parts[g] - column * row)
        inv[pl.ds(r0, b), :] = parts[1]
        for g in range(2, width):
            solved[pl.ds(r0, b), (g - 2) * P_SIZE : (g - 1) * P_SIZE] = parts[g]
        pieces = [split3(x) for x in parts]
        h, m, l = pieces[0]
        left = jnp.concatenate([h, h, m, h, m, l], axis=0)
        h, m, l = (jnp.concatenate([x[n] for x in pieces], axis=1) for n in range(3))
        right = jnp.concatenate([h, m, h, l, m, h], axis=0)
        work[...] -= lax.dot_general(left, right, FIRST, preferred_element_type=F32)
        if beside is not None:
            beside(k)
        return carry

    lax.fori_loop(first, last, step, 0)


def kernel(
    shape,
    state_hbm, cen_hbm, half_hbm, rad_hbm, order_hbm, var_hbm,
    out,
    ints, var,
    e_all, foot, tap, col_c, col_r, var_b, root_b, work, inv, solved, wts, p1, p1_b,
    part, rs, ag, cpart, crs, cag, sizes,
    in_s, e_s, x_s,
):
    n_slab, n_mem, n_sub = shape
    n = n_slab * n_sub
    total = n * n_mem
    own, rows = state_hbm.shape
    part_rows = rows // n_mem

    mi = lax.axis_index("mem")
    me = lax.axis_index("slab") * n_sub + lax.axis_index("sub")

    def peer(red, mem):
        return {"slab": lax.div(red, n_sub), "sub": lax.rem(red, n_sub), "mem": mem}

    def peer_of(off):
        red = lax.rem(me + lax.rem(off, n), n)
        mem = lax.rem(mi + lax.div(off, n), n_mem)
        return red, mem

    def remote(src, dst, send, recv, device):
        return pltpu.make_async_remote_copy(
            src_ref=src, dst_ref=dst, send_sem=send, recv_sem=recv,
            device_id=device, device_id_type=pl.DeviceIdType.MESH,
        )

    def wait_sent(ref, sem):
        remote(ref, ref, sem, sem, peer(me, mi)).wait_send()

    def wait_recv(ref, sem):
        remote(ref, ref, sem, sem, peer(me, mi)).wait_recv()

    small = [
        pltpu.make_async_copy(a, ints.at[i], in_s.at[0])
        for i, a in enumerate((cen_hbm, half_hbm, rad_hbm, order_hbm))
    ]
    var_copy = pltpu.make_async_copy(var_hbm, var, in_s.at[1])
    state_copy = pltpu.make_async_copy(state_hbm, e_all.at[mi], in_s.at[2])
    for copy in small:
        copy.start()
    var_copy.start()
    state_copy.start()

    barrier = pltpu.get_barrier_semaphore()

    def greet(off):
        red, mem = peer_of(off)
        pl.semaphore_signal(
            barrier, inc=1, device_id=peer(red, mem), device_id_type=pl.DeviceIdType.MESH
        )

    each(1, total, greet)
    pltpu.make_async_copy(ints, ints, in_s.at[0]).wait()
    var_copy.wait()

    n_obs = BATCHES * P_SIZE
    picked = jnp.broadcast_to(ints[3].astype(F32), (P_SIZE, n_obs)).T.astype(jnp.int32)
    lane = lax.broadcasted_iota(jnp.int32, (n_obs, P_SIZE), 1)
    masks = [picked == lane + h * P_SIZE for h in range(BATCHES)]

    def pick(ref):
        value = ref[...].astype(F32)
        chosen = 0.0
        for h in range(BATCHES):
            chosen = chosen + jnp.where(masks[h], value[:, h * P_SIZE : (h + 1) * P_SIZE], 0.0)
        return jnp.sum(chosen, axis=1, keepdims=True)

    center = pick(ints.at[0]) - (me * rows).astype(F32)
    width = pick(ints.at[1])
    variance = pick(var)
    col_c[...] = jnp.broadcast_to(center, (n_obs, P_SIZE))
    col_r[...] = jnp.broadcast_to(1.0 / pick(ints.at[2]), (n_obs, P_SIZE))
    var_b[...] = jnp.broadcast_to(variance, (n_obs, P_SIZE))
    root_b[...] = jnp.broadcast_to(jnp.sqrt(variance), (n_obs, P_SIZE))
    steep = -2.0 / (width * width)
    height = 1.0 / jnp.sqrt(width)

    def rows_of(mem):
        return pl.ds(pl.multiple_of(mem * part_rows, part_rows), part_rows)

    my_rows = rows_of(mi)

    def e_copy(off, q):
        to = lax.rem(mi + off, n_mem)
        at = rows_of(lax.rem(to + q, n_mem))
        k = 0 if q == 0 else 2
        return remote(
            state_hbm.at[:, at], e_all.at[mi, :, at], e_s.at[k], e_s.at[k + 1], peer(me, to)
        )

    def project(b):
        lo = b * P_SIZE

        def foot_tile(t, carry):
            at = pl.multiple_of(t * 256, 256)
            row = lax.broadcasted_iota(jnp.int32, (P_SIZE, 256), 1) + at
            distance = row.astype(F32) - center[lo : lo + P_SIZE]
            shape_f = jnp.exp(distance * distance * steep[lo : lo + P_SIZE]) - FLOOR
            shape_f = jnp.maximum(shape_f, 0.0) * height[lo : lo + P_SIZE]
            foot[lo : lo + P_SIZE, pl.ds(at, 256)] = shape_f.astype(BF16)
            return carry

        lax.fori_loop(0, rows // 256, foot_tile, 0)
        if b == 0:
            state_copy.wait()
        sums = lax.dot_general(
            foot[lo : lo + P_SIZE, :], e_all[mi], LAST, preferred_element_type=F32
        )
        part[b] = sums.reshape(part.shape[1:])

    class Sum:
        def __init__(self, size, index, device, source, target, result, everyone, sem, flat, span):
            self.size, self.index, self.device = size, index, device
            self.source, self.target, self.result, self.everyone = source, target, result, everyone
            self.sem, self.flat, self.span = sem, flat, span
            self.owners = source.shape[0]
            self.stride = size // self.owners
            self.mine = lax.div(index, self.stride)

        def if_owner(self, body, owner=True):
            if self.stride == 1:
                if owner:
                    body()
            else:
                pl.when((lax.rem(self.index, self.stride) == 0) == owner)(body)

        def out_copy(self, off):
            o = lax.rem(self.mine + off, self.owners)
            return remote(
                self.source.at[o], self.target.at[self.index],
                self.sem.at[0], self.sem.at[1], self.device(o * self.stride),
            )

        def start(self):
            each(1, self.owners, lambda off: self.out_copy(off).start())
            self.if_owner(lambda: self.out_copy(0).start(), False)

        def gather_copy(self, off):
            block = self.result(mi, self.mine)
            return remote(
                block, block, self.sem.at[2], self.sem.at[3], peer(*peer_of(off))
            )

        def finish(self):
            def body():
                wait_recv(self.target.at[pl.ds(0, self.size - 1)], self.sem.at[1])
                block = self.result(mi, self.mine)
                if self.size <= 16:
                    value = self.source[self.mine]
                    for off in range(1, self.size):
                        value = value + self.target[lax.rem(self.index + off, self.size)]
                    block[...] = value
                else:
                    block[...] = self.source[self.mine]

                    def add(off):
                        block[...] += self.target[lax.rem(self.index + off, self.size)]

                    each(1, self.size, add)
                each(1, total, lambda off: self.gather_copy(off).start())

            self.if_owner(body)

        def gather(self):
            count = (n_mem if self.everyone else 1) * self.owners
            self.if_owner(lambda: wait_recv(self.flat.at[pl.ds(0, count - 1)], self.sem.at[3]))
            self.if_owner(lambda: wait_recv(self.flat.at[pl.ds(0, count)], self.sem.at[3]), False)

        def sent(self):
            self.if_owner(
                lambda: wait_sent(self.source.at[pl.ds(0, self.owners - 1)], self.sem.at[0])
            )
            self.if_owner(lambda: wait_sent(self.source, self.sem.at[0]), False)
            self.if_owner(lambda: wait_sent(self.span.at[pl.ds(0, total - 1)], self.sem.at[2]))

    owners = part.shape[1]
    projections = [
        Sum(
            n, me, lambda i: peer(i, mi), part.at[b], rs.at[b],
            lambda mem, o, b=b: ag.at[b, mem * owners + o], True, x_s.at[b], ag.at[b], sizes,
        )
        for b in range(BATCHES)
    ]
    changes = Sum(
        total, mi * n + me, lambda i: peer(lax.rem(i, n), lax.div(i, n)), cpart, crs,
        lambda mem, o: cag.at[o], False, x_s.at[BATCHES], cag, crs,
    )
    project(0)
    pl.semaphore_wait(barrier, total - 1)
    projections[0].start()
    each(1, n_mem, lambda off: e_copy(off, 0).start())
    project(1)
    projections[1].start()
    projections[0].finish()
    for q in range(1, n_mem):
        each(1, n_mem, lambda off: e_copy(off, q).start())

    def slot(b, s):
        return ag[b, s * owners : (s + 1) * owners].reshape(P_SIZE, own)

    def load_work(columns, extra, b):
        cov = 0.0
        for s in range(n_mem):
            cov = cov + lax.dot_general(
                columns[s], columns[s], LAST, precision=HIGH, preferred_element_type=F32
            )
        r = lax.broadcasted_iota(jnp.int32, (P_SIZE, P_SIZE), 0)
        eye = r == lax.broadcasted_iota(jnp.int32, (P_SIZE, P_SIZE), 1)
        v = var_b[b * P_SIZE : (b + 1) * P_SIZE, :]
        work[:, :P_SIZE] = cov * (1.0 / (M - 1)) + jnp.where(eye, v, 0.0)
        work[:, P_SIZE : 2 * P_SIZE] = jnp.where(eye, 1.0, 0.0)
        lo = 2 * P_SIZE
        for x in extra:
            work[:, lo : lo + own] = x
            lo += own

    def taper(b, first, count):
        lo = b * P_SIZE
        row = lax.broadcasted_iota(jnp.int32, (P_SIZE, count), 1) + first
        c = jnp.concatenate([col_c[lo : lo + P_SIZE, :]] * (count // P_SIZE), axis=1)
        r = jnp.concatenate([col_r[lo : lo + P_SIZE, :]] * (count // P_SIZE), axis=1)
        near = jnp.maximum(1.0 - jnp.abs(row.astype(F32) - c) * r, 0.0)
        return near * near * (1.0 / (M - 1))

    projections[0].gather()
    first = [slot(0, s) for s in range(n_mem)]
    first_b = [x.astype(BF16) for x in first]

    def cross(which):
        mem = lax.rem(mi + which, n_mem)
        at = rows_of(mem)
        product = 0.0
        for s in range(n_mem):
            product = product + jnp.dot(first_b[s], e_all[s, :, at], preferred_element_type=F32)
        value = (taper(0, mem * part_rows, part_rows) * product).astype(BF16)
        tap[:, at] = value
        return value

    wait_recv(e_all.at[pl.ds(0, n_mem - 1), :, pl.ds(0, part_rows)], e_s.at[1])

    change = lax.dot_general(
        foot[P_SIZE : 2 * P_SIZE, my_rows], cross(0), LAST, preferred_element_type=F32
    )
    cpart[...] = change.reshape(cpart.shape)
    changes.start()
    projections[1].finish()

    load_work(first, first, 0)
    root_0 = root_b.at[pl.ds(0, P_SIZE)]
    sweep(work, inv, solved, root_0, 0, SPLIT)
    changes.finish()
    sweep(work, inv, solved, root_0, SPLIT)

    def weights(count):
        return lax.dot_general(
            solved[:, :count], inv[...], FIRST, precision=HIGH, preferred_element_type=F32
        ).astype(BF16)

    wts[...] = weights(M)

    wait_recv(
        e_all.at[pl.ds(0, n_mem - 1), :, pl.ds(0, (n_mem - 1) * part_rows)], e_s.at[3]
    )
    for q in range(1, n_mem):
        cross(q)
    def update(s):
        moved = jnp.dot(wts[s * own : (s + 1) * own, :], tap[...], preferred_element_type=F32)
        e_all[s] = (e_all[s].astype(F32) - moved).astype(BF16)

    for s in range(n_mem):
        update(s)

    projections[1].gather()
    changes.gather()
    c_full = jnp.concatenate(split3(cag[...].reshape(P_SIZE, P_SIZE)), axis=0)
    moved = lax.dot_general(c_full, wts[...], LAST, preferred_element_type=F32)
    moved = moved[:P_SIZE] + (moved[P_SIZE : 2 * P_SIZE] + moved[2 * P_SIZE :])
    second = []
    for s in range(n_mem):
        value = slot(1, s) - moved[:, s * own : (s + 1) * own]
        p1[s] = value
        p1_b[s] = value.astype(BF16)
        second.append(value)

    alone = own % P_SIZE == 0
    load_work(second, [p1[mi]] if alone else second, 1)

    def cross1(k):
        size = rows * BLOCK // P_SIZE
        at = pl.ds(pl.multiple_of(k * size, size), size)
        product = 0.0
        for s in range(n_mem):
            product = product + jnp.dot(p1_b[s], e_all[s, :, at], preferred_element_type=F32)
        tap[:, at] = (taper(1, k * size, size) * product).astype(BF16)

    used = 2 * P_SIZE + (own if alone else M)
    sweep(
        work.at[:, pl.ds(0, used)], inv, solved, root_b.at[pl.ds(P_SIZE, P_SIZE)], beside=cross1
    )
    if alone:
        own_w = weights(own)
    else:
        wts[...] = weights(M)
        own_w = wts[pl.ds(pl.multiple_of(mi * own, own), own), :]

    moved = jnp.dot(own_w, tap[...], preferred_element_type=F32)
    out[...] = (e_all[mi].astype(F32) - moved).astype(BF16)

    wait_sent(e_all.at[pl.ds(0, n_mem - 1), :, pl.ds(0, part_rows)], e_s.at[0])
    wait_sent(e_all.at[pl.ds(0, n_mem - 1), :, pl.ds(0, (n_mem - 1) * part_rows)], e_s.at[2])
    for x in projections + [changes]:
        x.sent()


def on_device(shape, state, centers, half_width, radius, order, obs_var):
    n_slab, n_mem, n_sub = shape
    own, rows = state.shape
    n = n_slab * n_sub
    total = n * n_mem
    owners = min(n, 8)
    chunk = P_SIZE // owners
    c_owners = min(total, 16)
    c_chunk = P_SIZE // c_owners
    n_obs = BATCHES * P_SIZE
    operands = (state,) + tuple(
        x[None, :] for x in (centers, half_width, radius, order, obs_var)
    )
    hbm = pl.BlockSpec(memory_space=pltpu.HBM)
    vmem = pl.BlockSpec(memory_space=pltpu.VMEM)
    return pl.pallas_call(
        functools.partial(kernel, shape),
        out_shape=pltpu.VMEM((own, rows), BF16),
        in_specs=[hbm] * 6,
        out_specs=vmem,
        scratch_shapes=[
            pltpu.VMEM((4, 1, n_obs), jnp.int32),
            pltpu.VMEM((1, n_obs), F32),
            pltpu.VMEM((n_mem, own, rows), BF16),
            pltpu.VMEM((n_obs, rows), BF16),
            pltpu.VMEM((P_SIZE, rows), BF16),
            pltpu.VMEM((n_obs, P_SIZE), F32),
            pltpu.VMEM((n_obs, P_SIZE), F32),
            pltpu.VMEM((n_obs, P_SIZE), F32),
            pltpu.VMEM((n_obs, P_SIZE), F32),
            pltpu.VMEM((P_SIZE, 2 * P_SIZE + M), F32),
            pltpu.VMEM((P_SIZE, P_SIZE), F32),
            pltpu.VMEM((P_SIZE, M), F32),
            pltpu.VMEM((M, P_SIZE), BF16),
            pltpu.VMEM((n_mem, P_SIZE, own), F32),
            pltpu.VMEM((n_mem, P_SIZE, own), BF16),
            pltpu.VMEM((BATCHES, owners, chunk, own), F32),
            pltpu.VMEM((BATCHES, n, chunk, own), F32),
            pltpu.VMEM((BATCHES, n_mem * owners, chunk, own), F32),
            pltpu.VMEM((c_owners, c_chunk, P_SIZE), F32),
            pltpu.VMEM((total, c_chunk, P_SIZE), F32),
            pltpu.VMEM((c_owners, c_chunk, P_SIZE), F32),
            pltpu.VMEM((total, chunk, own), F32),
            pltpu.SemaphoreType.DMA((3,)),
            pltpu.SemaphoreType.DMA((4,)),
            pltpu.SemaphoreType.DMA((BATCHES + 1, 4)),
        ],
        compiler_params=pltpu.CompilerParams(
            collective_id=0, has_side_effects=True, vmem_limit_bytes=40 * 1024 * 1024
        ),
    )(*(pltpu.with_memory_space_constraint(x, pltpu.HBM) for x in operands))


def solution(mesh):
    shape = (mesh.shape["slab"], mesh.shape["mem"], mesh.shape["sub"])
    placed = (P("mem", ("grp", "slab", "sub")), P("grp"), P("grp"), P("grp"), P("grp"), P("grp"))
    return jax.shard_map(
        functools.partial(on_device, shape),
        mesh=mesh,
        in_specs=placed,
        out_specs=P("mem", ("grp", "slab", "sub")),
        check_vma=False,
    )
```

```python
import functools
import math

import jax
import jax.numpy as jnp
from jax import lax
from jax.experimental import pallas as pl
from jax.experimental.pallas import tpu as pltpu
from jax.sharding import PartitionSpec as P

M = 256
P_SIZE = 128
BATCHES = 2
BLOCK = 32

FLOOR = math.exp(-2.0)
F32 = jnp.float32
BF16 = jnp.bfloat16
HIGH = lax.Precision.HIGHEST
LAST = (((1,), (1,)), ((), ()))
FIRST = (((0,), (0,)), ((), ()))


def each(start, stop, body):
    if stop - start <= 16:
        for i in range(start, stop):
            body(i)
    else:

        def step(i, carry):
            body(i)
            return carry

        lax.fori_loop(start, stop, step, 0)


def split3(x):
    high = x.astype(BF16)
    rest = x - high.astype(F32)
    mid = rest.astype(BF16)
    low = (rest - mid.astype(F32)).astype(BF16)
    return high, mid, low


def block(work, inv, solved, root, k):
    b = BLOCK
    size = b // 8
    width = work.shape[1] // P_SIZE
    r0 = k * b

    def at(v):
        return pl.ds(r0 + 8 * v, 8)

    def spread(x, i):
        return jnp.broadcast_to(x[i : i + 1, :], (8, P_SIZE))

    row = lax.broadcasted_iota(jnp.int32, (8, P_SIZE), 0)
    lane = lax.broadcasted_iota(jnp.int32, (8, P_SIZE), 1) - r0
    parts = [
        [work[at(v), g * P_SIZE : (g + 1) * P_SIZE] for v in range(size)] for g in range(width)
    ]
    roots = [root[at(v), :] for v in range(size)]
    cols = [
        {
            v: jnp.broadcast_to(parts[0][v][:, r0 + j : r0 + j + 1], (8, P_SIZE))
            for v in range(j // 8, size)
        }
        for j in range(b)
    ]
    inside = (lane >= 0) & (lane < b)
    for v in range(size):
        unit = jnp.where(lane == row + 8 * v, 1.0, 0.0)
        parts[0][v] = jnp.where(inside, unit, parts[0][v])
    pivots = [jnp.ones((8, P_SIZE), F32)] * size
    for j in range(b):
        top, jj = j // 8, j % 8
        column = cols[j]
        pivot = spread(column[top], jj)
        scale = lax.rsqrt(pivot)
        plain = scale * scale
        mixed = scale / (pivot * scale + spread(roots[top], jj))
        pivots[top] = jnp.where(row == jj, column[top], pivots[top])
        below = dict(column)
        below[top] = jnp.where(row > jj, column[top], 0.0)
        first = {v: x * plain for v, x in below.items()}
        other = {v: x * mixed for v, x in below.items()}
        for i in range(j + 1, b):
            s = spread(column[i // 8], i % 8)
            for v in range(i // 8, size):
                cols[i][v] = cols[i][v] - first[v] * s
        for g in range(width):
            line = spread(parts[g][top], jj)
            for v in range(top, size):
                parts[g][v] = parts[g][v] - (other if g else first)[v] * line
    for v in range(size):
        scale = lax.rsqrt(pivots[v])
        mixed = 1.0 / (pivots[v] * scale + roots[v])
        for g in range(width):
            parts[g][v] = parts[g][v] * (mixed if g else scale)
        inv[at(v), :] = jnp.where(lane < b, parts[0][v], 0.0)
        for g in range(1, width):
            solved[at(v), (g - 1) * P_SIZE : g * P_SIZE] = parts[g][v]
    lo = r0 + b
    if lo == P_SIZE:
        return
    pieces = [split3(jnp.concatenate(x, axis=0)) for x in parts]
    h, m, l = pieces[0]
    left = jnp.concatenate([h, h, m, h, m, l], axis=0)
    h, m, l = (jnp.concatenate([x[n] for x in pieces], axis=1) for n in range(3))
    right = jnp.concatenate([h, m, h, l, m, h], axis=0)
    change = lax.dot_general(left, right, FIRST, preferred_element_type=F32)[lo:]
    lane = lax.broadcasted_iota(jnp.int32, (P_SIZE - lo, P_SIZE), 1) - r0
    old = jnp.where((lane >= 0) & (lane < b), 0.0, work[lo:, :P_SIZE])
    work[lo:, :P_SIZE] = old - change[:, :P_SIZE]
    work[lo:, P_SIZE:] -= change[:, P_SIZE:]


def kernel(
    shape,
    state_hbm, cen_hbm, half_hbm, rad_hbm, order_hbm, var_hbm,
    out,
    ints, var,
    e_all, foot, tap, col_c, col_r, var_b, root_b, work, inv, solved, wts, p1, p1_b,
    part, rs, ag, ag_b, cpart, crs, cag, sizes, sizes_b,
    in_s, e_s, x_s,
):
    n_slab, n_mem, n_sub = shape
    n = n_slab * n_sub
    total = n * n_mem
    own, rows = state_hbm.shape
    part_rows = rows // n_mem

    mi = lax.axis_index("mem")
    me = lax.axis_index("slab") * n_sub + lax.axis_index("sub")

    def peer(red, mem):
        return {"slab": lax.div(red, n_sub), "sub": lax.rem(red, n_sub), "mem": mem}

    def peer_of(off):
        red = lax.rem(me + lax.rem(off, n), n)
        mem = lax.rem(mi + lax.div(off, n), n_mem)
        return red, mem

    def remote(src, dst, send, recv, device):
        return pltpu.make_async_remote_copy(
            src_ref=src, dst_ref=dst, send_sem=send, recv_sem=recv,
            device_id=device, device_id_type=pl.DeviceIdType.MESH,
        )

    def wait_sent(ref, sem):
        remote(ref, ref, sem, sem, peer(me, mi)).wait_send()

    def wait_recv(ref, sem):
        remote(ref, ref, sem, sem, peer(me, mi)).wait_recv()

    small = [
        pltpu.make_async_copy(a, ints.at[i], in_s.at[0])
        for i, a in enumerate((cen_hbm, half_hbm, rad_hbm, order_hbm))
    ]
    var_copy = pltpu.make_async_copy(var_hbm, var, in_s.at[1])
    state_copy = pltpu.make_async_copy(state_hbm, e_all.at[mi], in_s.at[2])
    for copy in small:
        copy.start()
    var_copy.start()
    state_copy.start()

    barrier = pltpu.get_barrier_semaphore()

    def greet(off):
        red, mem = peer_of(off)
        pl.semaphore_signal(
            barrier, inc=1, device_id=peer(red, mem), device_id_type=pl.DeviceIdType.MESH
        )

    each(1, total, greet)
    pltpu.make_async_copy(ints, ints, in_s.at[0]).wait()
    var_copy.wait()

    n_obs = BATCHES * P_SIZE
    picked = jnp.broadcast_to(ints[3].astype(F32), (P_SIZE, n_obs)).T.astype(jnp.int32)
    lane = lax.broadcasted_iota(jnp.int32, (n_obs, P_SIZE), 1)
    masks = [picked == lane + h * P_SIZE for h in range(BATCHES)]

    def pick(ref):
        value = ref[...].astype(F32)
        chosen = 0.0
        for h in range(BATCHES):
            chosen = chosen + jnp.where(masks[h], value[:, h * P_SIZE : (h + 1) * P_SIZE], 0.0)
        return jnp.sum(chosen, axis=1, keepdims=True)

    center = pick(ints.at[0]) - (me * rows).astype(F32)
    width = pick(ints.at[1])
    variance = pick(var)
    col_c[...] = jnp.broadcast_to(center, (n_obs, P_SIZE))
    col_r[...] = jnp.broadcast_to(1.0 / pick(ints.at[2]), (n_obs, P_SIZE))
    var_b[...] = jnp.broadcast_to(variance, (n_obs, P_SIZE))
    root_b[...] = jnp.broadcast_to(jnp.sqrt(variance), (n_obs, P_SIZE))
    steep = -2.0 / (width * width)
    height = 1.0 / jnp.sqrt(width)

    def rows_of(mem):
        return pl.ds(pl.multiple_of(mem * part_rows, part_rows), part_rows)

    my_rows = rows_of(mi)

    half_rows = part_rows // 2

    def half_of(mem, c):
        return pl.ds(pl.multiple_of(mem * part_rows + c * half_rows, half_rows), half_rows)

    def e_copy(off):
        to = lax.rem(mi + off, n_mem)
        at = rows_of(to)
        return remote(
            state_hbm.at[:, at], e_all.at[mi, :, at], e_s.at[0], e_s.at[1], peer(me, to)
        )

    def rest_copy(off, c):
        to = lax.rem(mi + lax.rem(off, n_mem - 1) + 1, n_mem)
        at = half_of(lax.rem(to + lax.div(off, n_mem - 1) + 1, n_mem), c)
        return remote(
            state_hbm.at[:, at], e_all.at[mi, :, at], e_s.at[2 + 2 * c], e_s.at[3 + 2 * c],
            peer(me, to),
        )

    def send_rest(c):
        each(0, (n_mem - 1) * (n_mem - 1), lambda off: rest_copy(off, c).start())

    rest = e_all.at[pl.ds(0, n_mem - 1), :, pl.ds(0, (n_mem - 1) * half_rows)]

    def project(b):
        lo = b * P_SIZE

        def foot_tile(t, carry):
            at = pl.multiple_of(t * 256, 256)
            row = lax.broadcasted_iota(jnp.int32, (P_SIZE, 256), 1) + at
            distance = row.astype(F32) - center[lo : lo + P_SIZE]
            shape_f = jnp.exp(distance * distance * steep[lo : lo + P_SIZE]) - FLOOR
            shape_f = jnp.maximum(shape_f, 0.0) * height[lo : lo + P_SIZE]
            foot[lo : lo + P_SIZE, pl.ds(at, 256)] = shape_f.astype(BF16)
            return carry

        lax.fori_loop(0, rows // 256, foot_tile, 0)
        if b == 0:
            state_copy.wait()
        sums = lax.dot_general(
            foot[lo : lo + P_SIZE, :], e_all[mi], LAST, preferred_element_type=F32
        )
        part[b] = sums.reshape(part.shape[1:])

    class Sum:
        def __init__(self, size, index, device, source, target, result, everyone, sem, flat, span, high=None):
            self.size, self.index, self.device = size, index, device
            self.source, self.target, self.result, self.everyone = source, target, result, everyone
            self.sem, self.flat, self.span, self.high = sem, flat, span, high
            self.owners = source.shape[0]
            self.stride = size // self.owners
            self.mine = lax.div(index, self.stride)

        def if_owner(self, body, owner=True):
            if self.stride == 1:
                if owner:
                    body()
            else:
                pl.when((lax.rem(self.index, self.stride) == 0) == owner)(body)

        def out_copy(self, off):
            o = lax.rem(self.mine + off, self.owners)
            return remote(
                self.source.at[o], self.target.at[self.index],
                self.sem.at[0], self.sem.at[1], self.device(o * self.stride),
            )

        def start(self):
            each(1, self.owners, lambda off: self.out_copy(off).start())
            self.if_owner(lambda: self.out_copy(0).start(), False)

        def gather_copy(self, off):
            block = self.result(mi, self.mine)
            return remote(
                block, block, self.sem.at[2], self.sem.at[3], peer(*peer_of(off))
            )

        def high_copy(self, off):
            block = self.high.at[mi * self.owners + self.mine]
            return remote(
                block, block, self.sem.at[4], self.sem.at[5], peer(*peer_of(off))
            )

        def finish(self):
            def body():
                wait_recv(self.target.at[pl.ds(0, self.size - 1)], self.sem.at[1])
                block = self.result(mi, self.mine)
                if self.size <= 16:
                    value = self.source[self.mine]
                    for off in range(1, self.size):
                        value = value + self.target[lax.rem(self.index + off, self.size)]
                    block[...] = value
                else:
                    block[...] = self.source[self.mine]

                    def add(off):
                        block[...] += self.target[lax.rem(self.index + off, self.size)]

                    each(1, self.size, add)
                if self.high is not None:
                    value = block[...]
                    high = value.astype(BF16)
                    self.high[mi * self.owners + self.mine] = high
                    each(1, total, lambda off: self.high_copy(off).start())
                    block[...] = value - high.astype(F32)
                each(1, total, lambda off: self.gather_copy(off).start())

            self.if_owner(body)

        def gather(self, flat=None, sem=3):
            flat = self.flat if flat is None else flat
            count = (n_mem if self.everyone else 1) * self.owners
            self.if_owner(lambda: wait_recv(flat.at[pl.ds(0, count - 1)], self.sem.at[sem]))
            self.if_owner(lambda: wait_recv(flat.at[pl.ds(0, count)], self.sem.at[sem]), False)

        def gather_high(self):
            self.gather(self.high, 5)

        def sent(self):
            self.if_owner(
                lambda: wait_sent(self.source.at[pl.ds(0, self.owners - 1)], self.sem.at[0])
            )
            self.if_owner(lambda: wait_sent(self.source, self.sem.at[0]), False)
            self.if_owner(lambda: wait_sent(self.span.at[pl.ds(0, total - 1)], self.sem.at[2]))
            if self.high is not None:
                self.if_owner(lambda: wait_sent(sizes_b.at[pl.ds(0, total - 1)], self.sem.at[4]))

    owners = part.shape[1]
    projections = [
        Sum(
            n, me, lambda i: peer(i, mi), part.at[b], rs.at[b],
            lambda mem, o, b=b: ag.at[b, mem * owners + o], True, x_s.at[b], ag.at[b], sizes,
            ag_b if b == 0 else None,
        )
        for b in range(BATCHES)
    ]
    changes = Sum(
        total, mi * n + me, lambda i: peer(lax.rem(i, n), lax.div(i, n)), cpart, crs,
        lambda mem, o: cag.at[o], False, x_s.at[BATCHES], cag, crs,
    )
    project(0)
    pl.semaphore_wait(barrier, total - 1)
    projections[0].start()
    each(1, n_mem, lambda off: e_copy(off).start())
    project(1)
    projections[1].start()
    projections[0].finish()
    send_rest(0)

    def slot(b, s):
        return ag[b, s * owners : (s + 1) * owners].reshape(P_SIZE, own)

    def load_work(columns, extra, b):
        cov = 0.0
        for s in range(n_mem):
            cov = cov + lax.dot_general(
                columns[s], columns[s], LAST, precision=HIGH, preferred_element_type=F32
            )
        r = lax.broadcasted_iota(jnp.int32, (P_SIZE, P_SIZE), 0)
        eye = r == lax.broadcasted_iota(jnp.int32, (P_SIZE, P_SIZE), 1)
        v = var_b[b * P_SIZE : (b + 1) * P_SIZE, :]
        work[:, :P_SIZE] = cov * (1.0 / (M - 1)) + jnp.where(eye, v, 0.0)
        lo = P_SIZE
        for x in extra:
            work[:, lo : lo + own] = x
            lo += own

    def taper(b, first, count):
        lo = b * P_SIZE
        row = lax.broadcasted_iota(jnp.int32, (P_SIZE, count), 1) + first
        c = jnp.concatenate([col_c[lo : lo + P_SIZE, :]] * (count // P_SIZE), axis=1)
        r = jnp.concatenate([col_r[lo : lo + P_SIZE, :]] * (count // P_SIZE), axis=1)
        near = jnp.maximum(1.0 - jnp.abs(row.astype(F32) - c) * r, 0.0)
        return near * near * (1.0 / (M - 1))

    projections[0].gather_high()
    first_b = [ag_b[s * owners : (s + 1) * owners].reshape(P_SIZE, own) for s in range(n_mem)]

    def cross(b, left, at, size):
        product = 0.0
        for s in range(n_mem):
            product = product + jnp.dot(left[s], e_all[s, :, at], preferred_element_type=F32)
        value = (taper(b, at.start, size) * product).astype(BF16)
        tap[:, at] = value
        return value

    def update(at):
        for s in range(n_mem):
            moved = jnp.dot(
                wts[s * own : (s + 1) * own, :], tap[:, at], preferred_element_type=F32
            )
            e_all[s, :, at] = (e_all[s, :, at].astype(F32) - moved).astype(BF16)

    wait_recv(e_all.at[pl.ds(0, n_mem - 1), :, pl.ds(0, part_rows)], e_s.at[1])

    change = lax.dot_general(
        foot[P_SIZE : 2 * P_SIZE, my_rows], cross(0, first_b, my_rows, part_rows),
        LAST, preferred_element_type=F32,
    )
    cpart[...] = change.reshape(cpart.shape)
    changes.start()
    projections[1].finish()

    projections[0].gather()
    first = [first_b[s].astype(F32) + slot(0, s) for s in range(n_mem)]
    load_work(first, first, 0)
    root_0 = root_b.at[pl.ds(0, P_SIZE)]
    blocks = P_SIZE // BLOCK
    for k in range(blocks // 2):
        block(work, inv, solved, root_0, k)
    changes.finish()
    send_rest(1)
    for k in range(blocks // 2, blocks):
        block(work, inv, solved, root_0, k)

    def weights(count):
        return lax.dot_general(
            solved[:, :count], inv[...], FIRST, precision=HIGH, preferred_element_type=F32
        ).astype(BF16)

    wts[...] = weights(M)

    def others(c):
        return [half_of(lax.rem(mi + q, n_mem), c) for q in range(1, n_mem)]

    update(my_rows)
    wait_recv(rest, e_s.at[3])
    for at in others(0):
        cross(0, first_b, at, half_rows)
        update(at)

    projections[1].gather()
    changes.gather()
    c_full = jnp.concatenate(split3(cag[...].reshape(P_SIZE, P_SIZE)), axis=0)
    moved = lax.dot_general(c_full, wts[...], LAST, preferred_element_type=F32)
    moved = moved[:P_SIZE] + (moved[P_SIZE : 2 * P_SIZE] + moved[2 * P_SIZE :])
    second = []
    for s in range(n_mem):
        value = slot(1, s) - moved[:, s * own : (s + 1) * own]
        p1[s] = value
        p1_b[s] = value.astype(BF16)
        second.append(value)

    alone = own % P_SIZE == 0
    load_work(second, [p1[mi]] if alone else second, 1)

    def beside(k):
        if k < 2:
            tiles = [half_of(mi, k)]
        elif k < 4:
            tiles = others(k - 2)
        else:
            tiles = []
        for at in tiles:
            if k == 3:
                cross(0, first_b, at, half_rows)
                update(at)
            cross(1, p1_b, at, half_rows)

    used = P_SIZE + (own if alone else M)
    for k in range(blocks):
        if k == 3:
            wait_recv(rest, e_s.at[5])
        block(
            work.at[:, pl.ds(0, used)], inv, solved, root_b.at[pl.ds(P_SIZE, P_SIZE)], k
        )
        beside(k)
    if alone:
        own_w = weights(own)
    else:
        wts[...] = weights(M)
        own_w = wts[pl.ds(pl.multiple_of(mi * own, own), own), :]

    moved = jnp.dot(own_w, tap[...], preferred_element_type=F32)
    out[...] = (e_all[mi].astype(F32) - moved).astype(BF16)

    wait_sent(e_all.at[pl.ds(0, n_mem - 1), :, pl.ds(0, part_rows)], e_s.at[0])
    wait_sent(rest, e_s.at[2])
    wait_sent(rest, e_s.at[4])
    for x in projections + [changes]:
        x.sent()


def on_device(shape, state, centers, half_width, radius, order, obs_var):
    n_slab, n_mem, n_sub = shape
    own, rows = state.shape
    n = n_slab * n_sub
    total = n * n_mem
    owners = min(n, 8)
    chunk = P_SIZE // owners
    c_owners = min(total, 16)
    c_chunk = P_SIZE // c_owners
    n_obs = BATCHES * P_SIZE
    operands = (state,) + tuple(
        x[None, :] for x in (centers, half_width, radius, order, obs_var)
    )
    hbm = pl.BlockSpec(memory_space=pltpu.HBM)
    vmem = pl.BlockSpec(memory_space=pltpu.VMEM)
    return pl.pallas_call(
        functools.partial(kernel, shape),
        out_shape=pltpu.VMEM((own, rows), BF16),
        in_specs=[hbm] * 6,
        out_specs=vmem,
        scratch_shapes=[
            pltpu.VMEM((4, 1, n_obs), jnp.int32),
            pltpu.VMEM((1, n_obs), F32),
            pltpu.VMEM((n_mem, own, rows), BF16),
            pltpu.VMEM((n_obs, rows), BF16),
            pltpu.VMEM((P_SIZE, rows), BF16),
            pltpu.VMEM((n_obs, P_SIZE), F32),
            pltpu.VMEM((n_obs, P_SIZE), F32),
            pltpu.VMEM((n_obs, P_SIZE), F32),
            pltpu.VMEM((n_obs, P_SIZE), F32),
            pltpu.VMEM((P_SIZE, P_SIZE + M), F32),
            pltpu.VMEM((P_SIZE, P_SIZE), F32),
            pltpu.VMEM((P_SIZE, M), F32),
            pltpu.VMEM((M, P_SIZE), BF16),
            pltpu.VMEM((n_mem, P_SIZE, own), F32),
            pltpu.VMEM((n_mem, P_SIZE, own), BF16),
            pltpu.VMEM((BATCHES, owners, chunk, own), F32),
            pltpu.VMEM((BATCHES, n, chunk, own), F32),
            pltpu.VMEM((BATCHES, n_mem * owners, chunk, own), F32),
            pltpu.VMEM((n_mem * owners, chunk, own), BF16),
            pltpu.VMEM((c_owners, c_chunk, P_SIZE), F32),
            pltpu.VMEM((total, c_chunk, P_SIZE), F32),
            pltpu.VMEM((c_owners, c_chunk, P_SIZE), F32),
            pltpu.VMEM((total, chunk, own), F32),
            pltpu.VMEM((total, chunk, own), BF16),
            pltpu.SemaphoreType.DMA((3,)),
            pltpu.SemaphoreType.DMA((6,)),
            pltpu.SemaphoreType.DMA((BATCHES + 1, 6)),
        ],
        compiler_params=pltpu.CompilerParams(
            collective_id=0, has_side_effects=True, vmem_limit_bytes=40 * 1024 * 1024
        ),
    )(*(pltpu.with_memory_space_constraint(x, pltpu.HBM) for x in operands))


def solution(mesh):
    shape = (mesh.shape["slab"], mesh.shape["mem"], mesh.shape["sub"])
    placed = (P("mem", ("grp", "slab", "sub")), P("grp"), P("grp"), P("grp"), P("grp"), P("grp"))
    return jax.shard_map(
        functools.partial(on_device, shape),
        mesh=mesh,
        in_specs=placed,
        out_specs=P("mem", ("grp", "slab", "sub")),
        check_vma=False,
    )
```

```python
import functools
import math

import jax
import jax.numpy as jnp
from jax import lax
from jax.experimental import pallas as pl
from jax.experimental.pallas import tpu as pltpu
from jax.sharding import PartitionSpec as P

M = 256
P_SIZE = 128
BATCHES = 2
BLOCK = 32
PANEL = 16
TILES = 4

FLOOR = math.exp(-2.0)
F32 = jnp.float32
BF16 = jnp.bfloat16
HIGH = lax.Precision.HIGHEST
LAST = (((1,), (1,)), ((), ()))
FIRST = (((0,), (0,)), ((), ()))


def each(start, stop, body):
    if stop - start <= 16:
        for i in range(start, stop):
            body(i)
    else:

        def step(i, carry):
            body(i)
            return carry

        lax.fori_loop(start, stop, step, 0)


def split3(x):
    high = x.astype(BF16)
    rest = x - high.astype(F32)
    mid = rest.astype(BF16)
    low = (rest - mid.astype(F32)).astype(BF16)
    return high, mid, low


def block(work, inv, solved, root, k):
    b = BLOCK
    size = b // 8
    width = work.shape[1] // P_SIZE
    r0 = k * b

    def at(v):
        return pl.ds(r0 + 8 * v, 8)

    def spread(x, i):
        return jnp.broadcast_to(x[i : i + 1, :], (8, P_SIZE))

    row = lax.broadcasted_iota(jnp.int32, (8, P_SIZE), 0)
    lane = lax.broadcasted_iota(jnp.int32, (8, P_SIZE), 1) - r0
    parts = [
        [work[at(v), g * P_SIZE : (g + 1) * P_SIZE] for v in range(size)] for g in range(width)
    ]
    roots = [root[at(v), :] for v in range(size)]
    pivots = [jnp.ones((8, P_SIZE), F32)] * size
    for j in range(0, b, 2):
        top, jj = j // 8, j % 8
        if j % PANEL == 0:
            cols = {
                i: {
                    v: jnp.broadcast_to(parts[0][v][:, r0 + i : r0 + i + 1], (8, P_SIZE))
                    for v in range(i // 8, size)
                }
                for i in range(j, j + PANEL)
            }
            inside = (lane >= j) & (lane < j + PANEL)
            for v in range(top, size):
                unit = jnp.where(lane == row + 8 * v, 1.0, 0.0) if 8 * v < j + PANEL else 0.0
                parts[0][v] = jnp.where(inside, unit, parts[0][v])
        c0, c1 = cols[j], cols[j + 1]
        p, q, r = spread(c0[top], jj), spread(c0[top], jj + 1), spread(c1[top], jj + 1)
        det = p * r - q * q
        inverse = 1.0 / det
        root_p, root_d = lax.rsqrt(p), lax.rsqrt(det)
        cross = q * root_p
        mix0 = 1.0 / (p * root_p + spread(roots[top], jj))
        mix1 = 1.0 / (det * root_d * root_p + spread(roots[top], jj + 1))
        below = cross * mix0
        after = root_d * root_p * mix1
        ahead = root_p * mix0
        left, right, left_m, right_m = {}, {}, {}, {}
        for v in range(top, size):
            x, y = r * c0[v] - q * c1[v], p * c1[v] - q * c0[v]
            left[v], right[v] = x * inverse, y * inverse
            right_m[v] = y * after
            left_m[v] = c0[v] * ahead - right_m[v] * below
        last = row == jj + 1
        done = row <= jj + 1
        for x, y, z in ((left, right, cross * root_p), (left_m, right_m, below)):
            x[top] = jnp.where(done, jnp.where(last, z, 0.0), x[top])
            y[top] = jnp.where(done, 0.0, y[top])
        pivots[top] = jnp.where(row == jj, p, pivots[top])
        pivots[top] = jnp.where(last, det * root_p * root_p, pivots[top])
        for i in range(j + 2, j - j % PANEL + PANEL):
            s0, s1 = spread(c0[i // 8], i % 8), spread(c1[i // 8], i % 8)
            for v in range(i // 8, size):
                cols[i][v] = cols[i][v] - left[v] * s0 - right[v] * s1
        for g in range(width):
            s0, s1 = spread(parts[g][top], jj), spread(parts[g][top], jj + 1)
            x, y = (left_m, right_m) if g else (left, right)
            for v in range(top, size):
                parts[g][v] = parts[g][v] - x[v] * s0 - y[v] * s1
    for v in range(size):
        scale = lax.rsqrt(pivots[v])
        mixed = 1.0 / (pivots[v] * scale + roots[v])
        for g in range(width):
            parts[g][v] = parts[g][v] * (mixed if g else scale)
        ahead = (lane >= (8 * v // PANEL + 1) * PANEL) & (lane < b)
        parts[0][v] = jnp.where(ahead, 0.0, parts[0][v])
        inv[at(v), :] = jnp.where(lane < b, parts[0][v], 0.0)
        for g in range(1, width):
            solved[at(v), (g - 1) * P_SIZE : g * P_SIZE] = parts[g][v]
    lo = r0 + b
    if lo == P_SIZE:
        return
    pieces = [split3(jnp.concatenate(x, axis=0)) for x in parts]
    h, m, l = pieces[0]
    left = jnp.concatenate([h, h, m, h, m, l], axis=0)
    h, m, l = (jnp.concatenate([x[n] for x in pieces], axis=1) for n in range(3))
    right = jnp.concatenate([h, m, h, l, m, h], axis=0)
    change = lax.dot_general(left, right, FIRST, preferred_element_type=F32)[lo:]
    lane = lax.broadcasted_iota(jnp.int32, (P_SIZE - lo, P_SIZE), 1) - r0
    old = jnp.where((lane >= 0) & (lane < b), 0.0, work[lo:, :P_SIZE])
    work[lo:, :P_SIZE] = old - change[:, :P_SIZE]
    work[lo:, P_SIZE:] -= change[:, P_SIZE:]


def kernel(
    shape,
    state_hbm, cen_hbm, half_hbm, rad_hbm, order_hbm, var_hbm,
    out,
    ints, var,
    e_all, foot, tap, tapers, col_c, col_r, var_b, root_b, work, inv, solved, wts, p1, p1_b,
    part, rs, ag, ag_b, cpart, crs, cag, sizes, sizes_b,
    in_s, e_s, x_s,
):
    n_slab, n_mem, n_sub = shape
    n = n_slab * n_sub
    total = n * n_mem
    own, rows = state_hbm.shape

    mi = lax.axis_index("mem")
    me = lax.axis_index("slab") * n_sub + lax.axis_index("sub")

    def peer(red, mem):
        return {"slab": lax.div(red, n_sub), "sub": lax.rem(red, n_sub), "mem": mem}

    def peer_of(off):
        red = lax.rem(me + lax.rem(off, n), n)
        mem = lax.rem(mi + lax.div(off, n), n_mem)
        return red, mem

    def remote(src, dst, send, recv, device):
        return pltpu.make_async_remote_copy(
            src_ref=src, dst_ref=dst, send_sem=send, recv_sem=recv,
            device_id=device, device_id_type=pl.DeviceIdType.MESH,
        )

    def wait_sent(ref, sem):
        remote(ref, ref, sem, sem, peer(me, mi)).wait_send()

    def wait_recv(ref, sem):
        remote(ref, ref, sem, sem, peer(me, mi)).wait_recv()

    small = [
        pltpu.make_async_copy(a, ints.at[i], in_s.at[0])
        for i, a in enumerate((cen_hbm, half_hbm, rad_hbm, order_hbm))
    ]
    var_copy = pltpu.make_async_copy(var_hbm, var, in_s.at[1])
    state_copy = pltpu.make_async_copy(state_hbm, e_all.at[mi], in_s.at[2])
    for copy in small:
        copy.start()
    var_copy.start()
    state_copy.start()

    barrier = pltpu.get_barrier_semaphore()

    def greet(off):
        red, mem = peer_of(off)
        pl.semaphore_signal(
            barrier, inc=1, device_id=peer(red, mem), device_id_type=pl.DeviceIdType.MESH
        )

    each(1, total, greet)
    pltpu.make_async_copy(ints, ints, in_s.at[0]).wait()
    var_copy.wait()

    n_obs = BATCHES * P_SIZE
    picked = jnp.broadcast_to(ints[3].astype(F32), (P_SIZE, n_obs)).T.astype(jnp.int32)
    lane = lax.broadcasted_iota(jnp.int32, (n_obs, P_SIZE), 1)
    masks = [picked == lane + h * P_SIZE for h in range(BATCHES)]

    def pick(ref):
        value = ref[...].astype(F32)
        chosen = 0.0
        for h in range(BATCHES):
            chosen = chosen + jnp.where(masks[h], value[:, h * P_SIZE : (h + 1) * P_SIZE], 0.0)
        return jnp.sum(chosen, axis=1, keepdims=True)

    center = pick(ints.at[0]) - (me * rows).astype(F32)
    width = pick(ints.at[1])
    variance = pick(var)
    col_c[...] = jnp.broadcast_to(center, (n_obs, P_SIZE))
    col_r[...] = jnp.broadcast_to(1.0 / pick(ints.at[2]), (n_obs, P_SIZE))
    var_b[...] = jnp.broadcast_to(variance, (n_obs, P_SIZE))
    root_b[...] = jnp.broadcast_to(jnp.sqrt(variance), (n_obs, P_SIZE))
    steep = -2.0 / (width * width)
    height = 1.0 / jnp.sqrt(width)

    size = rows // TILES

    def tile(c):
        return pl.ds(c * size, size)

    def e_copy(off, c):
        return remote(
            state_hbm.at[:, tile(c)], e_all.at[mi, :, tile(c)], e_s.at[0], e_s.at[1 + c],
            peer(me, lax.rem(mi + off, n_mem)),
        )

    def send_state(c):
        each(1, n_mem, lambda off: e_copy(off, c).start())

    def wait_state(c):
        wait_recv(e_all.at[pl.ds(0, n_mem - 1), :, tile(c)], e_s.at[1 + c])

    def project(b):
        lo = b * P_SIZE

        def foot_tile(t, carry):
            at = pl.multiple_of(t * 256, 256)
            row = lax.broadcasted_iota(jnp.int32, (P_SIZE, 256), 1) + at
            distance = row.astype(F32) - center[lo : lo + P_SIZE]
            shape_f = jnp.exp(distance * distance * steep[lo : lo + P_SIZE]) - FLOOR
            shape_f = jnp.maximum(shape_f, 0.0) * height[lo : lo + P_SIZE]
            foot[lo : lo + P_SIZE, pl.ds(at, 256)] = shape_f.astype(BF16)
            return carry

        lax.fori_loop(0, rows // 256, foot_tile, 0)
        if b == 0:
            state_copy.wait()
        sums = lax.dot_general(
            foot[lo : lo + P_SIZE, :], e_all[mi], LAST, preferred_element_type=F32
        )
        part[b] = sums.reshape(part.shape[1:])

    class Sum:
        def __init__(self, size, index, device, source, target, result, everyone, sem, flat, span, high=None):
            self.size, self.index, self.device = size, index, device
            self.source, self.target, self.result, self.everyone = source, target, result, everyone
            self.sem, self.flat, self.span, self.high = sem, flat, span, high
            self.owners = source.shape[0]
            self.stride = size // self.owners
            self.mine = lax.div(index, self.stride)

        def if_owner(self, body, owner=True):
            if self.stride == 1:
                if owner:
                    body()
            else:
                pl.when((lax.rem(self.index, self.stride) == 0) == owner)(body)

        def out_copy(self, off):
            o = lax.rem(self.mine + off, self.owners)
            return remote(
                self.source.at[o], self.target.at[self.index],
                self.sem.at[0], self.sem.at[1], self.device(o * self.stride),
            )

        def start(self):
            each(1, self.owners, lambda off: self.out_copy(off).start())
            self.if_owner(lambda: self.out_copy(0).start(), False)

        def gather_copy(self, off):
            block = self.result(mi, self.mine)
            return remote(
                block, block, self.sem.at[2], self.sem.at[3], peer(*peer_of(off))
            )

        def high_copy(self, off):
            block = self.high.at[self.mine]
            to = self.device(lax.rem(self.index + off, self.size))
            return remote(block, block, self.sem.at[4], self.sem.at[5], to)

        def finish(self):
            def body():
                wait_recv(self.target.at[pl.ds(0, self.size - 1)], self.sem.at[1])
                block = self.result(mi, self.mine)
                if self.size <= 16:
                    value = self.source[self.mine]
                    for off in range(1, self.size):
                        value = value + self.target[lax.rem(self.index + off, self.size)]
                    block[...] = value
                else:
                    block[...] = self.source[self.mine]

                    def add(off):
                        block[...] += self.target[lax.rem(self.index + off, self.size)]

                    each(1, self.size, add)
                if self.high is not None:
                    self.high[self.mine] = block[...].astype(BF16)
                    each(1, self.size, lambda off: self.high_copy(off).start())
                each(1, total, lambda off: self.gather_copy(off).start())

            self.if_owner(body)

        def arrived(self, flat, count, sem):
            self.if_owner(lambda: wait_recv(flat.at[pl.ds(0, count - 1)], self.sem.at[sem]))
            self.if_owner(lambda: wait_recv(flat.at[pl.ds(0, count)], self.sem.at[sem]), False)

        def gather(self):
            self.arrived(self.flat, (n_mem if self.everyone else 1) * self.owners, 3)

        def gather_high(self):
            self.arrived(self.high, self.owners, 5)

        def sent(self):
            self.if_owner(
                lambda: wait_sent(self.source.at[pl.ds(0, self.owners - 1)], self.sem.at[0])
            )
            self.if_owner(lambda: wait_sent(self.source, self.sem.at[0]), False)
            self.if_owner(lambda: wait_sent(self.span.at[pl.ds(0, total - 1)], self.sem.at[2]))
            if self.high is not None:
                self.if_owner(
                    lambda: wait_sent(sizes_b.at[pl.ds(0, self.size - 1)], self.sem.at[4])
                )

    owners = part.shape[1]
    projections = [
        Sum(
            n, me, lambda i: peer(i, mi), part.at[b], rs.at[b],
            lambda mem, o, b=b: ag.at[b, mem * owners + o], True, x_s.at[b], ag.at[b], sizes,
            ag_b if b == 0 else None,
        )
        for b in range(BATCHES)
    ]
    changes = Sum(
        total, mi * n + me, lambda i: peer(lax.rem(i, n), lax.div(i, n)), cpart, crs,
        lambda mem, o: cag.at[o], False, x_s.at[BATCHES], cag, crs,
    )
    project(0)
    pl.semaphore_wait(barrier, total - 1)
    projections[0].start()
    send_state(0)
    project(1)
    projections[1].start()
    projections[0].finish()
    send_state(1)

    def slot(b, s):
        return ag[b, s * owners : (s + 1) * owners].reshape(P_SIZE, own)

    def load_work(columns, extra, b):
        cov = 0.0
        for s in range(n_mem):
            cov = cov + lax.dot_general(
                columns[s], columns[s], LAST, precision=HIGH, preferred_element_type=F32
            )
        r = lax.broadcasted_iota(jnp.int32, (P_SIZE, P_SIZE), 0)
        eye = r == lax.broadcasted_iota(jnp.int32, (P_SIZE, P_SIZE), 1)
        v = var_b[b * P_SIZE : (b + 1) * P_SIZE, :]
        work[:, :P_SIZE] = cov * (1.0 / (M - 1)) + jnp.where(eye, v, 0.0)
        lo = P_SIZE
        for x in extra:
            work[:, lo : lo + own] = x
            lo += own

    def taper(b, at):
        lo = b * P_SIZE
        row = lax.broadcasted_iota(jnp.int32, (P_SIZE, size), 1) + at.start
        c = jnp.concatenate([col_c[lo : lo + P_SIZE, :]] * (size // P_SIZE), axis=1)
        r = jnp.concatenate([col_r[lo : lo + P_SIZE, :]] * (size // P_SIZE), axis=1)
        near = jnp.maximum(1.0 - jnp.abs(row.astype(F32) - c) * r, 0.0)
        return near * near * (1.0 / (M - 1))

    for b in range(BATCHES):
        for c in range(TILES):
            tapers[b, :, tile(c)] = taper(b, tile(c))

    projections[0].gather_high()

    mine_b = ag_b[...].reshape(P_SIZE, own)
    change = 0.0
    for c in range(TILES):
        product = jnp.dot(mine_b, e_all[mi, :, tile(c)], preferred_element_type=F32)
        product = tapers[0, :, tile(c)] * product
        high = product.astype(BF16)
        low = (product - high.astype(F32)).astype(BF16)
        for x in (high, low):
            change = change + lax.dot_general(
                foot[P_SIZE : 2 * P_SIZE, tile(c)], x, LAST, preferred_element_type=F32
            )
    cpart[...] = change.reshape(cpart.shape)
    changes.start()
    projections[1].finish()
    send_state(2)

    projections[0].gather()
    first = [slot(0, s) for s in range(n_mem)]
    load_work(first, first, 0)
    root_0 = root_b.at[pl.ds(0, P_SIZE)]
    blocks = P_SIZE // BLOCK
    for k in range(blocks // 2):
        block(work, inv, solved, root_0, k)
    changes.finish()
    send_state(3)
    for k in range(blocks // 2, blocks):
        block(work, inv, solved, root_0, k)

    def weights(count):
        return lax.dot_general(
            solved[:, :count], inv[...], FIRST, precision=HIGH, preferred_element_type=F32
        ).astype(BF16)

    wts[...] = weights(M)
    first_b = [slot(0, s).astype(BF16) for s in range(n_mem)]

    def cross(b, left, at):
        product = 0.0
        for s in range(n_mem):
            product = product + jnp.dot(left[s], e_all[s, :, at], preferred_element_type=F32)
        tap[:, at] = (tapers[b, :, at] * product).astype(BF16)

    def update(at):
        cross(0, first_b, at)
        for s in range(n_mem):
            moved = jnp.dot(
                wts[s * own : (s + 1) * own, :], tap[:, at], preferred_element_type=F32
            )
            e_all[s, :, at] = (e_all[s, :, at].astype(F32) - moved).astype(BF16)

    for c in range(TILES - 1):
        wait_state(c)
        update(tile(c))

    projections[1].gather()
    changes.gather()
    c_full = jnp.concatenate(split3(cag[...].reshape(P_SIZE, P_SIZE)), axis=0)
    moved = lax.dot_general(c_full, wts[...], LAST, preferred_element_type=F32)
    moved = moved[:P_SIZE] + (moved[P_SIZE : 2 * P_SIZE] + moved[2 * P_SIZE :])
    second = []
    for s in range(n_mem):
        value = slot(1, s) - moved[:, s * own : (s + 1) * own]
        p1[s] = value
        p1_b[s] = value.astype(BF16)
        second.append(value)

    alone = own % P_SIZE == 0
    load_work(second, [p1[mi]] if alone else second, 1)

    used = P_SIZE + (own if alone else M)
    for k in range(blocks):
        if k == TILES - 1:
            wait_state(k)
            update(tile(k))
        block(
            work.at[:, pl.ds(0, used)], inv, solved, root_b.at[pl.ds(P_SIZE, P_SIZE)], k
        )
        cross(1, p1_b, tile(k))
    if alone:
        own_w = weights(own)
    else:
        wts[...] = weights(M)
        own_w = wts[pl.ds(pl.multiple_of(mi * own, own), own), :]

    moved = jnp.dot(own_w, tap[...], preferred_element_type=F32)
    out[...] = (e_all[mi].astype(F32) - moved).astype(BF16)

    wait_sent(e_all.at[pl.ds(0, n_mem - 1)], e_s.at[0])
    for x in projections + [changes]:
        x.sent()


def on_device(shape, state, centers, half_width, radius, order, obs_var):
    n_slab, n_mem, n_sub = shape
    own, rows = state.shape
    n = n_slab * n_sub
    total = n * n_mem
    owners = min(n, 8)
    chunk = P_SIZE // owners
    c_owners = min(total, 16)
    c_chunk = P_SIZE // c_owners
    n_obs = BATCHES * P_SIZE
    operands = (state,) + tuple(
        x[None, :] for x in (centers, half_width, radius, order, obs_var)
    )
    hbm = pl.BlockSpec(memory_space=pltpu.HBM)
    vmem = pl.BlockSpec(memory_space=pltpu.VMEM)
    return pl.pallas_call(
        functools.partial(kernel, shape),
        out_shape=pltpu.VMEM((own, rows), BF16),
        in_specs=[hbm] * 6,
        out_specs=vmem,
        scratch_shapes=[
            pltpu.VMEM((4, 1, n_obs), jnp.int32),
            pltpu.VMEM((1, n_obs), F32),
            pltpu.VMEM((n_mem, own, rows), BF16),
            pltpu.VMEM((n_obs, rows), BF16),
            pltpu.VMEM((P_SIZE, rows), BF16),
            pltpu.VMEM((BATCHES, P_SIZE, rows), F32),
            pltpu.VMEM((n_obs, P_SIZE), F32),
            pltpu.VMEM((n_obs, P_SIZE), F32),
            pltpu.VMEM((n_obs, P_SIZE), F32),
            pltpu.VMEM((n_obs, P_SIZE), F32),
            pltpu.VMEM((P_SIZE, P_SIZE + M), F32),
            pltpu.VMEM((P_SIZE, P_SIZE), F32),
            pltpu.VMEM((P_SIZE, M), F32),
            pltpu.VMEM((M, P_SIZE), BF16),
            pltpu.VMEM((n_mem, P_SIZE, own), F32),
            pltpu.VMEM((n_mem, P_SIZE, own), BF16),
            pltpu.VMEM((BATCHES, owners, chunk, own), F32),
            pltpu.VMEM((BATCHES, n, chunk, own), F32),
            pltpu.VMEM((BATCHES, n_mem * owners, chunk, own), F32),
            pltpu.VMEM((owners, chunk, own), BF16),
            pltpu.VMEM((c_owners, c_chunk, P_SIZE), F32),
            pltpu.VMEM((total, c_chunk, P_SIZE), F32),
            pltpu.VMEM((c_owners, c_chunk, P_SIZE), F32),
            pltpu.VMEM((total, chunk, own), F32),
            pltpu.VMEM((n, chunk, own), BF16),
            pltpu.SemaphoreType.DMA((3,)),
            pltpu.SemaphoreType.DMA((1 + TILES,)),
            pltpu.SemaphoreType.DMA((BATCHES + 1, 6)),
        ],
        compiler_params=pltpu.CompilerParams(
            collective_id=0, has_side_effects=True, vmem_limit_bytes=40 * 1024 * 1024
        ),
    )(*(pltpu.with_memory_space_constraint(x, pltpu.HBM) for x in operands))


def solution(mesh):
    shape = (mesh.shape["slab"], mesh.shape["mem"], mesh.shape["sub"])
    placed = (P("mem", ("grp", "slab", "sub")), P("grp"), P("grp"), P("grp"), P("grp"), P("grp"))
    return jax.shard_map(
        functools.partial(on_device, shape),
        mesh=mesh,
        in_specs=placed,
        out_specs=P("mem", ("grp", "slab", "sub")),
        check_vma=False,
    )
```

```python
import functools
import math

import jax
import jax.numpy as jnp
from jax import lax
from jax.experimental import pallas as pl
from jax.experimental.pallas import tpu as pltpu
from jax.sharding import PartitionSpec as P

M = 256
P_SIZE = 128
BATCHES = 2
BLOCK = 32
PANEL = 16
TILES = 4

FLOOR = math.exp(-2.0)
F32 = jnp.float32
BF16 = jnp.bfloat16
HIGH = lax.Precision.HIGHEST
LAST = (((1,), (1,)), ((), ()))
FIRST = (((0,), (0,)), ((), ()))


def each(start, stop, body):
    if stop - start <= 16:
        for i in range(start, stop):
            body(i)
    else:

        def step(i, carry):
            body(i)
            return carry

        lax.fori_loop(start, stop, step, 0)


def split3(x):
    high = x.astype(BF16)
    rest = x - high.astype(F32)
    mid = rest.astype(BF16)
    low = (rest - mid.astype(F32)).astype(BF16)
    return high, mid, low


def block(work, inv, solved, root, k):
    b = BLOCK
    size = b // 8
    width = work.shape[1] // P_SIZE
    r0 = k * b

    def at(v):
        return pl.ds(r0 + 8 * v, 8)

    def spread(x, i):
        return jnp.broadcast_to(x[i : i + 1, :], (8, P_SIZE))

    row = lax.broadcasted_iota(jnp.int32, (8, P_SIZE), 0)
    lane = lax.broadcasted_iota(jnp.int32, (8, P_SIZE), 1) - r0
    parts = [
        [work[at(v), g * P_SIZE : (g + 1) * P_SIZE] for v in range(size)] for g in range(width)
    ]
    roots = [root[at(v), :] for v in range(size)]
    pivots = [jnp.ones((8, P_SIZE), F32)] * size
    for j in range(0, b, 2):
        top, jj = j // 8, j % 8
        if j % PANEL == 0:
            cols = {
                i: {
                    v: jnp.broadcast_to(parts[0][v][:, r0 + i : r0 + i + 1], (8, P_SIZE))
                    for v in range(i // 8, size)
                }
                for i in range(j, j + PANEL)
            }
            inside = (lane >= j) & (lane < j + PANEL)
            for v in range(top, size):
                unit = jnp.where(lane == row + 8 * v, 1.0, 0.0) if 8 * v < j + PANEL else 0.0
                parts[0][v] = jnp.where(inside, unit, parts[0][v])
        c0, c1 = cols[j], cols[j + 1]
        p, q, r = spread(c0[top], jj), spread(c0[top], jj + 1), spread(c1[top], jj + 1)
        det = p * r - q * q
        inverse = 1.0 / det
        root_p, root_d = lax.rsqrt(p), lax.rsqrt(det)
        cross = q * root_p
        mix0 = 1.0 / (p * root_p + spread(roots[top], jj))
        mix1 = 1.0 / (det * root_d * root_p + spread(roots[top], jj + 1))
        below = cross * mix0
        after = root_d * root_p * mix1
        ahead = root_p * mix0
        left, right, left_m, right_m = {}, {}, {}, {}
        for v in range(top, size):
            x, y = r * c0[v] - q * c1[v], p * c1[v] - q * c0[v]
            left[v], right[v] = x * inverse, y * inverse
            right_m[v] = y * after
            left_m[v] = c0[v] * ahead - right_m[v] * below
        last = row == jj + 1
        done = row <= jj + 1
        for x, y, z in ((left, right, cross * root_p), (left_m, right_m, below)):
            x[top] = jnp.where(done, jnp.where(last, z, 0.0), x[top])
            y[top] = jnp.where(done, 0.0, y[top])
        pivots[top] = jnp.where(row == jj, p, pivots[top])
        pivots[top] = jnp.where(last, det * root_p * root_p, pivots[top])
        for i in range(j + 2, j - j % PANEL + PANEL):
            s0, s1 = spread(c0[i // 8], i % 8), spread(c1[i // 8], i % 8)
            for v in range(i // 8, size):
                cols[i][v] = cols[i][v] - left[v] * s0 - right[v] * s1
        for g in range(width):
            s0, s1 = spread(parts[g][top], jj), spread(parts[g][top], jj + 1)
            x, y = (left_m, right_m) if g else (left, right)
            for v in range(top, size):
                parts[g][v] = parts[g][v] - x[v] * s0 - y[v] * s1
    for v in range(size):
        scale = lax.rsqrt(pivots[v])
        mixed = 1.0 / (pivots[v] * scale + roots[v])
        for g in range(width):
            parts[g][v] = parts[g][v] * (mixed if g else scale)
        ahead = (lane >= (8 * v // PANEL + 1) * PANEL) & (lane < b)
        parts[0][v] = jnp.where(ahead, 0.0, parts[0][v])
        inv[at(v), :] = jnp.where(lane < b, parts[0][v], 0.0)
        for g in range(1, width):
            solved[at(v), (g - 1) * P_SIZE : g * P_SIZE] = parts[g][v]
    lo = r0 + b
    if lo == P_SIZE:
        return
    pieces = [split3(jnp.concatenate(x, axis=0)) for x in parts]
    h, m, l = pieces[0]
    left = jnp.concatenate([h, h, m, h, m, l], axis=0)
    h, m, l = (jnp.concatenate([x[n] for x in pieces], axis=1) for n in range(3))
    right = jnp.concatenate([h, m, h, l, m, h], axis=0)
    change = lax.dot_general(left, right, FIRST, preferred_element_type=F32)[lo:]
    lane = lax.broadcasted_iota(jnp.int32, (P_SIZE - lo, P_SIZE), 1) - r0
    old = jnp.where((lane >= 0) & (lane < b), 0.0, work[lo:, :P_SIZE])
    work[lo:, :P_SIZE] = old - change[:, :P_SIZE]
    work[lo:, P_SIZE:] -= change[:, P_SIZE:]


def kernel(
    shape,
    state_hbm, cen_hbm, half_hbm, rad_hbm, order_hbm, var_hbm,
    out,
    ints, var,
    e_all, foot, tap, tapers, col_c, col_r, var_b, root_b, work, inv, solved, wts, p1, p1_b,
    part, rs, ag, ag_b, cpart, crs, cag, sizes, sizes_b,
    in_s, e_s, x_s,
):
    n_slab, n_mem, n_sub = shape
    n = n_slab * n_sub
    total = n * n_mem
    own, rows = state_hbm.shape

    mi = lax.axis_index("mem")
    slab, sub = lax.axis_index("slab"), lax.axis_index("sub")
    me = slab * n_sub + sub

    def peer(red, mem):
        return {"slab": lax.div(red, n_sub), "sub": lax.rem(red, n_sub), "mem": mem}

    def peer_of(off):
        red = lax.rem(me + lax.rem(off, n), n)
        mem = lax.rem(mi + lax.div(off, n), n_mem)
        return red, mem

    def remote(src, dst, send, recv, device):
        return pltpu.make_async_remote_copy(
            src_ref=src, dst_ref=dst, send_sem=send, recv_sem=recv,
            device_id=device, device_id_type=pl.DeviceIdType.MESH,
        )

    def wait_sent(ref, sem):
        remote(ref, ref, sem, sem, peer(me, mi)).wait_send()

    def wait_recv(ref, sem):
        remote(ref, ref, sem, sem, peer(me, mi)).wait_recv()

    small = [
        pltpu.make_async_copy(a, ints.at[i], in_s.at[0])
        for i, a in enumerate((cen_hbm, half_hbm, rad_hbm, order_hbm))
    ]
    var_copy = pltpu.make_async_copy(var_hbm, var, in_s.at[1])
    state_copy = pltpu.make_async_copy(state_hbm, e_all.at[mi], in_s.at[2])
    for copy in small:
        copy.start()
    var_copy.start()
    state_copy.start()

    barrier = pltpu.get_barrier_semaphore()

    def greet(off):
        red, mem = peer_of(off)
        pl.semaphore_signal(
            barrier, inc=1, device_id=peer(red, mem), device_id_type=pl.DeviceIdType.MESH
        )

    each(1, total, greet)
    pltpu.make_async_copy(ints, ints, in_s.at[0]).wait()
    var_copy.wait()

    n_obs = BATCHES * P_SIZE
    picked = jnp.broadcast_to(ints[3].astype(F32), (P_SIZE, n_obs)).T.astype(jnp.int32)
    lane = lax.broadcasted_iota(jnp.int32, (n_obs, P_SIZE), 1)
    masks = [picked == lane + h * P_SIZE for h in range(BATCHES)]

    def pick(ref):
        value = ref[...].astype(F32)
        chosen = 0.0
        for h in range(BATCHES):
            chosen = chosen + jnp.where(masks[h], value[:, h * P_SIZE : (h + 1) * P_SIZE], 0.0)
        return jnp.sum(chosen, axis=1, keepdims=True)

    center = pick(ints.at[0]) - (me * rows).astype(F32)
    width = pick(ints.at[1])
    variance = pick(var)
    col_c[...] = jnp.broadcast_to(center, (n_obs, P_SIZE))
    col_r[...] = jnp.broadcast_to(1.0 / pick(ints.at[2]), (n_obs, P_SIZE))
    var_b[...] = jnp.broadcast_to(variance, (n_obs, P_SIZE))
    root_b[...] = jnp.broadcast_to(jnp.sqrt(variance), (n_obs, P_SIZE))
    steep = -2.0 / (width * width)
    height = 1.0 / jnp.sqrt(width)

    size = rows // TILES

    def tile(c):
        return pl.ds(c * size, size)

    def e_copy(off, c):
        return remote(
            state_hbm.at[:, tile(c)], e_all.at[mi, :, tile(c)], e_s.at[0], e_s.at[1 + c],
            peer(me, lax.rem(mi + off, n_mem)),
        )

    def send_state(c):
        each(1, n_mem, lambda off: e_copy(off, c).start())

    def wait_state(c):
        wait_recv(e_all.at[pl.ds(0, n_mem - 1), :, tile(c)], e_s.at[1 + c])

    def project(b):
        lo = b * P_SIZE

        def foot_tile(t, carry):
            at = pl.multiple_of(t * 256, 256)
            row = lax.broadcasted_iota(jnp.int32, (P_SIZE, 256), 1) + at
            distance = row.astype(F32) - center[lo : lo + P_SIZE]
            shape_f = jnp.exp(distance * distance * steep[lo : lo + P_SIZE]) - FLOOR
            shape_f = jnp.maximum(shape_f, 0.0) * height[lo : lo + P_SIZE]
            foot[lo : lo + P_SIZE, pl.ds(at, 256)] = shape_f.astype(BF16)
            return carry

        lax.fori_loop(0, rows // 256, foot_tile, 0)
        if b == 0:
            state_copy.wait()
        sums = lax.dot_general(
            foot[lo : lo + P_SIZE, :], e_all[mi], LAST, preferred_element_type=F32
        )
        part[b] = sums.reshape(part.shape[1:])

    class Sum:
        def __init__(self, size, index, device, source, target, result, blocks, sem, base, span, high=None):
            self.size, self.index, self.device = size, index, device
            everyone = blocks is not None
            self.source, self.target, self.result, self.blocks = source, target, result, blocks
            self.everyone = everyone
            self.sems, self.base, self.span, self.high = sem, base, span, high
            self.owners = source.shape[0]
            self.stride = size // self.owners
            self.mine = lax.div(index, self.stride)
            self.relayed = everyone and self.stride == 1
            self.sends = (n_slab * n_mem if self.relayed else total) - 1
            self.handed = (n_sub - 1) * n_slab * n_mem

        def sem(self, k):
            return self.sems.at[self.base + k]

        def if_owner(self, body, owner=True):
            if self.stride == 1:
                if owner:
                    body()
            else:
                pl.when((lax.rem(self.index, self.stride) == 0) == owner)(body)

        def out_copy(self, off):
            o = lax.rem(self.mine + off, self.owners)
            return remote(
                self.source.at[o], self.target.at[self.index],
                self.sem(0), self.sem(1), self.device(o * self.stride),
            )

        def start(self):
            each(1, self.owners, lambda off: self.out_copy(off).start())
            self.if_owner(lambda: self.out_copy(0).start(), False)

        def gather_copy(self, off):
            block = self.result(mi, self.mine)
            to = peer(*peer_of(off))
            if self.relayed:
                to = {
                    "slab": lax.rem(slab + lax.rem(off, n_slab), n_slab),
                    "mem": lax.rem(mi + lax.div(off, n_slab), n_mem),
                }
            return remote(block, block, self.sem(2), self.sem(3), to)

        def relay_copy(self, off):
            blocks = self.blocks.at[:, sub]
            to = {"sub": lax.rem(sub + off, n_sub)}
            return remote(blocks, blocks, self.sem(4), self.sem(5), to)

        def relay(self):
            if self.relayed:
                wait_recv(self.span.at[pl.ds(0, self.sends)], self.sem(3))
                each(1, n_sub, lambda off: self.relay_copy(off).start())

        def high_copy(self, off):
            block = self.high.at[self.mine]
            to = self.device(lax.rem(self.index + off, self.size))
            return remote(block, block, self.sem(6), self.sem(7), to)

        def finish(self):
            def body():
                wait_recv(self.target.at[pl.ds(0, self.size - 1)], self.sem(1))
                block = self.result(mi, self.mine)
                if self.size <= 16:
                    value = self.source[self.mine]
                    for off in range(1, self.size):
                        value = value + self.target[lax.rem(self.index + off, self.size)]
                    block[...] = value
                else:
                    block[...] = self.source[self.mine]

                    def add(off):
                        block[...] += self.target[lax.rem(self.index + off, self.size)]

                    each(1, self.size, add)
                if self.high is not None:
                    self.high[self.mine] = block[...].astype(BF16)
                    each(1, self.size, lambda off: self.high_copy(off).start())
                each(1, self.sends + 1, lambda off: self.gather_copy(off).start())

            self.if_owner(body)

        def arrived(self, flat, count, sem):
            self.if_owner(lambda: wait_recv(flat.at[pl.ds(0, count - 1)], self.sem(sem)))
            self.if_owner(lambda: wait_recv(flat.at[pl.ds(0, count)], self.sem(sem)), False)

        def gather(self):
            if self.relayed:
                wait_recv(self.span.at[pl.ds(0, self.handed)], self.sem(5))
            else:
                self.arrived(self.span, (n_mem if self.everyone else 1) * self.owners, 3)

        def gather_high(self):
            self.arrived(self.high, self.owners, 7)

        def sent(self):
            self.if_owner(
                lambda: wait_sent(self.source.at[pl.ds(0, self.owners - 1)], self.sem(0))
            )
            self.if_owner(lambda: wait_sent(self.source, self.sem(0)), False)
            self.if_owner(lambda: wait_sent(self.span.at[pl.ds(0, self.sends)], self.sem(2)))
            if self.relayed:
                wait_sent(self.span.at[pl.ds(0, self.handed)], self.sem(4))
            if self.high is not None:
                self.if_owner(
                    lambda: wait_sent(sizes_b.at[pl.ds(0, self.size - 1)], self.sem(6))
                )

    owners = part.shape[1]
    projections = [
        Sum(
            n, me, lambda i: peer(i, mi), part.at[b], rs.at[b],
            lambda mem, o, b=b: ag.at[b, lax.div(mem * owners + o, n_sub), lax.rem(mem * owners + o, n_sub)],
            ag.at[b], x_s, 8 * b, sizes, ag_b if b == 0 else None,
        )
        for b in range(BATCHES)
    ]
    changes = Sum(
        total, mi * n + me, lambda i: peer(lax.rem(i, n), lax.div(i, n)), cpart, crs,
        lambda mem, o: cag.at[o], None, x_s, 14, crs,
    )
    project(0)
    pl.semaphore_wait(barrier, total - 1)
    projections[0].start()
    send_state(0)
    send_state(1)
    project(1)
    projections[1].start()
    projections[0].finish()
    send_state(2)

    def slot(b, s):
        step = owners // n_sub
        return ag[b, s * step : (s + 1) * step].reshape(P_SIZE, own)

    def load_work(columns, extra, b):
        h, m, l = (jnp.concatenate(x, axis=1) for x in zip(*(split3(x) for x in columns)))
        cov = lax.dot_general(
            jnp.concatenate([h, h, m, h, m, l], axis=1),
            jnp.concatenate([h, m, h, l, m, h], axis=1),
            LAST, preferred_element_type=F32,
        )
        r = lax.broadcasted_iota(jnp.int32, (P_SIZE, P_SIZE), 0)
        eye = r == lax.broadcasted_iota(jnp.int32, (P_SIZE, P_SIZE), 1)
        v = var_b[b * P_SIZE : (b + 1) * P_SIZE, :]
        work[:, :P_SIZE] = cov * (1.0 / (M - 1)) + jnp.where(eye, v, 0.0)
        lo = P_SIZE
        for x in extra:
            work[:, lo : lo + own] = x
            lo += own

    def taper(b, at):
        lo = b * P_SIZE
        row = lax.broadcasted_iota(jnp.int32, (P_SIZE, size), 1) + at.start
        c = jnp.concatenate([col_c[lo : lo + P_SIZE, :]] * (size // P_SIZE), axis=1)
        r = jnp.concatenate([col_r[lo : lo + P_SIZE, :]] * (size // P_SIZE), axis=1)
        near = jnp.maximum(1.0 - jnp.abs(row.astype(F32) - c) * r, 0.0)
        return near * near * (1.0 / (M - 1))

    for b in range(BATCHES):
        for c in range(TILES):
            tapers[b, :, tile(c)] = taper(b, tile(c))

    projections[0].gather_high()

    mine_b = ag_b[...].reshape(P_SIZE, own)
    change = 0.0
    for c in range(TILES):
        product = jnp.dot(mine_b, e_all[mi, :, tile(c)], preferred_element_type=F32)
        product = tapers[0, :, tile(c)] * product
        high = product.astype(BF16)
        low = (product - high.astype(F32)).astype(BF16)
        for x in (high, low):
            change = change + lax.dot_general(
                foot[P_SIZE : 2 * P_SIZE, tile(c)], x, LAST, preferred_element_type=F32
            )
    cpart[...] = change.reshape(cpart.shape)
    changes.start()
    projections[1].finish()

    projections[0].relay()
    projections[0].gather()
    first = [slot(0, s) for s in range(n_mem)]
    load_work(first, first, 0)
    root_0 = root_b.at[pl.ds(0, P_SIZE)]
    blocks = P_SIZE // BLOCK
    for k in range(blocks // 2):
        block(work, inv, solved, root_0, k)
        if k == 0:
            send_state(3)
    changes.finish()
    for k in range(blocks // 2, blocks):
        block(work, inv, solved, root_0, k)

    def weights(count):
        h, m, l = split3(solved[:, :count])
        left = jnp.concatenate([h, h, m, h, m, l], axis=0)
        h, m, l = split3(inv[...])
        right = jnp.concatenate([h, m, h, l, m, h], axis=0)
        return lax.dot_general(left, right, FIRST, preferred_element_type=F32).astype(BF16)

    wts[...] = weights(M)
    projections[1].relay()
    first_b = [slot(0, s).astype(BF16) for s in range(n_mem)]

    def cross(b, left, at):
        product = 0.0
        for s in range(n_mem):
            product = product + jnp.dot(left[s], e_all[s, :, at], preferred_element_type=F32)
        tap[:, at] = (tapers[b, :, at] * product).astype(BF16)

    def update(at):
        cross(0, first_b, at)
        for s in range(n_mem):
            moved = jnp.dot(
                wts[s * own : (s + 1) * own, :], tap[:, at], preferred_element_type=F32
            )
            e_all[s, :, at] = (e_all[s, :, at].astype(F32) - moved).astype(BF16)

    for c in range(TILES):
        wait_state(c)
        update(tile(c))

    projections[1].gather()
    changes.gather()
    c_full = jnp.concatenate(split3(cag[...].reshape(P_SIZE, P_SIZE)), axis=0)
    moved = lax.dot_general(c_full, wts[...], LAST, preferred_element_type=F32)
    moved = moved[:P_SIZE] + (moved[P_SIZE : 2 * P_SIZE] + moved[2 * P_SIZE :])
    second = []
    for s in range(n_mem):
        value = slot(1, s) - moved[:, s * own : (s + 1) * own]
        p1[s] = value
        p1_b[s] = value.astype(BF16)
        second.append(value)

    alone = own % P_SIZE == 0
    load_work(second, [p1[mi]] if alone else second, 1)

    used = P_SIZE + (own if alone else M)
    for k in range(blocks):
        block(
            work.at[:, pl.ds(0, used)], inv, solved, root_b.at[pl.ds(P_SIZE, P_SIZE)], k
        )
        cross(1, p1_b, tile(k))
    if alone:
        own_w = weights(own)
    else:
        wts[...] = weights(M)
        own_w = wts[pl.ds(pl.multiple_of(mi * own, own), own), :]

    moved = jnp.dot(own_w, tap[...], preferred_element_type=F32)
    out[...] = (e_all[mi].astype(F32) - moved).astype(BF16)

    wait_sent(e_all.at[pl.ds(0, n_mem - 1)], e_s.at[0])
    for x in projections + [changes]:
        x.sent()


def on_device(shape, state, centers, half_width, radius, order, obs_var):
    n_slab, n_mem, n_sub = shape
    own, rows = state.shape
    n = n_slab * n_sub
    total = n * n_mem
    owners = min(n, 8)
    chunk = P_SIZE // owners
    c_owners = min(total, 16)
    c_chunk = P_SIZE // c_owners
    n_obs = BATCHES * P_SIZE
    operands = (state,) + tuple(
        x[None, :] for x in (centers, half_width, radius, order, obs_var)
    )
    hbm = pl.BlockSpec(memory_space=pltpu.HBM)
    vmem = pl.BlockSpec(memory_space=pltpu.VMEM)
    return pl.pallas_call(
        functools.partial(kernel, shape),
        out_shape=pltpu.VMEM((own, rows), BF16),
        in_specs=[hbm] * 6,
        out_specs=vmem,
        scratch_shapes=[
            pltpu.VMEM((4, 1, n_obs), jnp.int32),
            pltpu.VMEM((1, n_obs), F32),
            pltpu.VMEM((n_mem, own, rows), BF16),
            pltpu.VMEM((n_obs, rows), BF16),
            pltpu.VMEM((P_SIZE, rows), BF16),
            pltpu.VMEM((BATCHES, P_SIZE, rows), F32),
            pltpu.VMEM((n_obs, P_SIZE), F32),
            pltpu.VMEM((n_obs, P_SIZE), F32),
            pltpu.VMEM((n_obs, P_SIZE), F32),
            pltpu.VMEM((n_obs, P_SIZE), F32),
            pltpu.VMEM((P_SIZE, P_SIZE + M), F32),
            pltpu.VMEM((P_SIZE, P_SIZE), F32),
            pltpu.VMEM((P_SIZE, M), F32),
            pltpu.VMEM((M, P_SIZE), BF16),
            pltpu.VMEM((n_mem, P_SIZE, own), F32),
            pltpu.VMEM((n_mem, P_SIZE, own), BF16),
            pltpu.VMEM((BATCHES, owners, chunk, own), F32),
            pltpu.VMEM((BATCHES, n, chunk, own), F32),
            pltpu.VMEM((BATCHES, n_mem * owners // n_sub, n_sub, chunk, own), F32),
            pltpu.VMEM((owners, chunk, own), BF16),
            pltpu.VMEM((c_owners, c_chunk, P_SIZE), F32),
            pltpu.VMEM((total, c_chunk, P_SIZE), F32),
            pltpu.VMEM((c_owners, c_chunk, P_SIZE), F32),
            pltpu.VMEM((total, chunk, own), F32),
            pltpu.VMEM((n, chunk, own), BF16),
            pltpu.SemaphoreType.DMA((3,)),
            pltpu.SemaphoreType.DMA((1 + TILES,)),
            pltpu.SemaphoreType.DMA((18,)),
        ],
        compiler_params=pltpu.CompilerParams(
            collective_id=0, has_side_effects=True, vmem_limit_bytes=40 * 1024 * 1024
        ),
    )(*(pltpu.with_memory_space_constraint(x, pltpu.HBM) for x in operands))


def solution(mesh):
    shape = (mesh.shape["slab"], mesh.shape["mem"], mesh.shape["sub"])
    placed = (P("mem", ("grp", "slab", "sub")), P("grp"), P("grp"), P("grp"), P("grp"), P("grp"))
    return jax.shard_map(
        functools.partial(on_device, shape),
        mesh=mesh,
        in_specs=placed,
        out_specs=P("mem", ("grp", "slab", "sub")),
        check_vma=False,
    )
```

```python
import functools
import math

import jax
import jax.numpy as jnp
from jax import lax
from jax.experimental import pallas as pl
from jax.experimental.pallas import tpu as pltpu
from jax.sharding import PartitionSpec as P

M = 256
P_SIZE = 128
BATCHES = 2
BLOCK = 32
PANEL = 16
TILES = 4

FLOOR = math.exp(-2.0)
F32 = jnp.float32
BF16 = jnp.bfloat16
HIGH = lax.Precision.HIGHEST
LAST = (((1,), (1,)), ((), ()))
FIRST = (((0,), (0,)), ((), ()))


def each(start, stop, body):
    if stop - start <= 16:
        for i in range(start, stop):
            body(i)
    else:

        def step(i, carry):
            body(i)
            return carry

        lax.fori_loop(start, stop, step, 0)


def split3(x):
    high = x.astype(BF16)
    rest = x - high.astype(F32)
    mid = rest.astype(BF16)
    low = (rest - mid.astype(F32)).astype(BF16)
    return high, mid, low


def block(work, inv, solved, root, k):
    b = BLOCK
    size = b // 8
    width = work.shape[1] // P_SIZE
    r0 = k * b

    def at(v):
        return pl.ds(r0 + 8 * v, 8)

    def spread(x, i):
        return jnp.broadcast_to(x[i : i + 1, :], (8, P_SIZE))

    row = lax.broadcasted_iota(jnp.int32, (8, P_SIZE), 0)
    lane = lax.broadcasted_iota(jnp.int32, (8, P_SIZE), 1) - r0
    parts = [
        [work[at(v), g * P_SIZE : (g + 1) * P_SIZE] for v in range(size)] for g in range(width)
    ]
    roots = [root[at(v), :] for v in range(size)]
    pivots = [jnp.ones((8, P_SIZE), F32)] * size
    for j in range(0, b, 2):
        top, jj = j // 8, j % 8
        if j % PANEL == 0:
            cols = {
                i: {
                    v: jnp.broadcast_to(parts[0][v][:, r0 + i : r0 + i + 1], (8, P_SIZE))
                    for v in range(i // 8, size)
                }
                for i in range(j, j + PANEL)
            }
            inside = (lane >= j) & (lane < j + PANEL)
            for v in range(top, size):
                unit = jnp.where(lane == row + 8 * v, 1.0, 0.0) if 8 * v < j + PANEL else 0.0
                parts[0][v] = jnp.where(inside, unit, parts[0][v])
        c0, c1 = cols[j], cols[j + 1]
        p, q, r = spread(c0[top], jj), spread(c0[top], jj + 1), spread(c1[top], jj + 1)
        det = p * r - q * q
        inverse = 1.0 / det
        root_p, root_d = lax.rsqrt(p), lax.rsqrt(det)
        cross = q * root_p
        mix0 = 1.0 / (p * root_p + spread(roots[top], jj))
        mix1 = 1.0 / (det * root_d * root_p + spread(roots[top], jj + 1))
        below = cross * mix0
        after = root_d * root_p * mix1
        ahead = root_p * mix0
        left, right, left_m, right_m = {}, {}, {}, {}
        for v in range(top, size):
            x, y = r * c0[v] - q * c1[v], p * c1[v] - q * c0[v]
            left[v], right[v] = x * inverse, y * inverse
            right_m[v] = y * after
            left_m[v] = c0[v] * ahead - right_m[v] * below
        last = row == jj + 1
        done = row <= jj + 1
        for x, y, z in ((left, right, cross * root_p), (left_m, right_m, below)):
            x[top] = jnp.where(done, jnp.where(last, z, 0.0), x[top])
            y[top] = jnp.where(done, 0.0, y[top])
        pivots[top] = jnp.where(row == jj, p, pivots[top])
        pivots[top] = jnp.where(last, det * root_p * root_p, pivots[top])
        for i in range(j + 2, j - j % PANEL + PANEL):
            s0, s1 = spread(c0[i // 8], i % 8), spread(c1[i // 8], i % 8)
            for v in range(i // 8, size):
                cols[i][v] = cols[i][v] - left[v] * s0 - right[v] * s1
        for g in range(width):
            s0, s1 = spread(parts[g][top], jj), spread(parts[g][top], jj + 1)
            x, y = (left_m, right_m) if g else (left, right)
            for v in range(top, size):
                parts[g][v] = parts[g][v] - x[v] * s0 - y[v] * s1
    for v in range(size):
        scale = lax.rsqrt(pivots[v])
        mixed = 1.0 / (pivots[v] * scale + roots[v])
        for g in range(width):
            parts[g][v] = parts[g][v] * (mixed if g else scale)
        ahead = (lane >= (8 * v // PANEL + 1) * PANEL) & (lane < b)
        parts[0][v] = jnp.where(ahead, 0.0, parts[0][v])
        inv[at(v), :] = jnp.where(lane < b, parts[0][v], 0.0)
        for g in range(1, width):
            solved[at(v), (g - 1) * P_SIZE : g * P_SIZE] = parts[g][v]
    lo = r0 + b
    if lo == P_SIZE:
        return
    pieces = [split3(jnp.concatenate(x, axis=0)) for x in parts]
    h, m, l = pieces[0]
    left = jnp.concatenate([h, h, m, h, m, l], axis=0)
    h, m, l = (jnp.concatenate([x[n] for x in pieces], axis=1) for n in range(3))
    right = jnp.concatenate([h, m, h, l, m, h], axis=0)
    change = lax.dot_general(left, right, FIRST, preferred_element_type=F32)[lo:]
    lane = lax.broadcasted_iota(jnp.int32, (P_SIZE - lo, P_SIZE), 1) - r0
    old = jnp.where((lane >= 0) & (lane < b), 0.0, work[lo:, :P_SIZE])
    work[lo:, :P_SIZE] = old - change[:, :P_SIZE]
    work[lo:, P_SIZE:] -= change[:, P_SIZE:]


def kernel(
    shape,
    state_hbm, cen_hbm, half_hbm, rad_hbm, order_hbm, var_hbm,
    out,
    ints, var,
    e_all, foot, tap, tapers, col_c, col_r, var_b, root_b, work, inv, solved, wts, p1, p1_b,
    part, rs, ag, ag_b, cpart, crs, cag, sizes, sizes_b,
    in_s, e_s, x_s,
):
    n_slab, n_mem, n_sub = shape
    n = n_slab * n_sub
    total = n * n_mem
    own, rows = state_hbm.shape

    mi = lax.axis_index("mem")
    slab, sub = lax.axis_index("slab"), lax.axis_index("sub")
    me = slab * n_sub + sub

    def peer(red, mem):
        return {"slab": lax.div(red, n_sub), "sub": lax.rem(red, n_sub), "mem": mem}

    def peer_of(off):
        red = lax.rem(me + lax.rem(off, n), n)
        mem = lax.rem(mi + lax.div(off, n), n_mem)
        return red, mem

    def remote(src, dst, send, recv, device):
        return pltpu.make_async_remote_copy(
            src_ref=src, dst_ref=dst, send_sem=send, recv_sem=recv,
            device_id=device, device_id_type=pl.DeviceIdType.MESH,
        )

    def wait_sent(ref, sem):
        remote(ref, ref, sem, sem, peer(me, mi)).wait_send()

    def wait_recv(ref, sem):
        remote(ref, ref, sem, sem, peer(me, mi)).wait_recv()

    small = [
        pltpu.make_async_copy(a, ints.at[i], in_s.at[0])
        for i, a in enumerate((cen_hbm, half_hbm, rad_hbm, order_hbm))
    ]
    var_copy = pltpu.make_async_copy(var_hbm, var, in_s.at[1])
    state_copy = pltpu.make_async_copy(state_hbm, e_all.at[mi], in_s.at[2])
    for copy in small:
        copy.start()
    var_copy.start()
    state_copy.start()

    barrier = pltpu.get_barrier_semaphore()

    def greet(off):
        red, mem = peer_of(off)
        pl.semaphore_signal(
            barrier, inc=1, device_id=peer(red, mem), device_id_type=pl.DeviceIdType.MESH
        )

    each(1, total, greet)
    pltpu.make_async_copy(ints, ints, in_s.at[0]).wait()
    var_copy.wait()

    n_obs = BATCHES * P_SIZE
    picked = jnp.broadcast_to(ints[3].astype(F32), (P_SIZE, n_obs)).T.astype(jnp.int32)
    lane = lax.broadcasted_iota(jnp.int32, (n_obs, P_SIZE), 1)
    masks = [picked == lane + h * P_SIZE for h in range(BATCHES)]

    def pick(ref):
        value = ref[...].astype(F32)
        chosen = 0.0
        for h in range(BATCHES):
            chosen = chosen + jnp.where(masks[h], value[:, h * P_SIZE : (h + 1) * P_SIZE], 0.0)
        return jnp.sum(chosen, axis=1, keepdims=True)

    center = pick(ints.at[0]) - (me * rows).astype(F32)
    width = pick(ints.at[1])
    variance = pick(var)
    col_c[...] = jnp.broadcast_to(center, (n_obs, P_SIZE))
    col_r[...] = jnp.broadcast_to(1.0 / pick(ints.at[2]), (n_obs, P_SIZE))
    var_b[...] = jnp.broadcast_to(variance, (n_obs, P_SIZE))
    root_b[...] = jnp.broadcast_to(jnp.sqrt(variance), (n_obs, P_SIZE))
    steep = -2.0 / (width * width)
    height = 1.0 / jnp.sqrt(width)

    size = rows // TILES

    def tile(c):
        return pl.ds(c * size, size)

    def e_copy(off, c):
        return remote(
            state_hbm.at[:, tile(c)], e_all.at[mi, :, tile(c)], e_s.at[0], e_s.at[1 + c],
            peer(me, lax.rem(mi + off, n_mem)),
        )

    def send_state(c):
        each(1, n_mem, lambda off: e_copy(off, c).start())

    def wait_state(c):
        wait_recv(e_all.at[pl.ds(0, n_mem - 1), :, tile(c)], e_s.at[1 + c])

    def project(b):
        lo = b * P_SIZE

        def foot_tile(t, carry):
            at = pl.multiple_of(t * 256, 256)
            row = lax.broadcasted_iota(jnp.int32, (P_SIZE, 256), 1) + at
            distance = row.astype(F32) - center[lo : lo + P_SIZE]
            shape_f = jnp.exp(distance * distance * steep[lo : lo + P_SIZE]) - FLOOR
            shape_f = jnp.maximum(shape_f, 0.0) * height[lo : lo + P_SIZE]
            foot[lo : lo + P_SIZE, pl.ds(at, 256)] = shape_f.astype(BF16)
            return carry

        lax.fori_loop(0, rows // 256, foot_tile, 0)
        if b == 0:
            state_copy.wait()
        sums = lax.dot_general(
            foot[lo : lo + P_SIZE, :], e_all[mi], LAST, preferred_element_type=F32
        )
        part[b] = sums.reshape(part.shape[1:])

    owners = per = part.shape[1]
    middle = (n - per) // 2

    class Sum:
        def __init__(self, size, index, device, source, target, result, blocks, sem, base, span, high=None):
            self.size, self.index, self.device = size, index, device
            everyone = blocks is not None
            self.source, self.target, self.result, self.blocks = source, target, result, blocks
            self.everyone = everyone
            self.sems, self.base, self.span, self.high = sem, base, span, high
            self.owners = source.shape[0]
            self.relayed = everyone
            self.mine = lax.rem(me + n * per - middle, per) + (0 if everyone else mi * per)
            self.sends = (n_slab * n_mem if everyone else total) - 1
            self.direct = n_mem * per // n_sub
            self.handed = (n_sub - 1) * self.direct

        def owner_of(self, o):
            return self.device(lax.div(o, per) * n + middle + lax.rem(o, per))

        def sem(self, k):
            return self.sems.at[self.base + k]

        def if_owner(self, body, owner=True):
            inside = jnp.logical_and(me >= middle, me < middle + per)
            pl.when(inside if owner else jnp.logical_not(inside))(body)

        def out_copy(self, off):
            o = lax.rem(self.mine + off, self.owners)
            return remote(
                self.source.at[o], self.target.at[self.index],
                self.sem(0), self.sem(1), self.owner_of(o),
            )

        def start(self):
            each(1, self.owners, lambda off: self.out_copy(off).start())
            self.if_owner(lambda: self.out_copy(0).start(), False)

        def gather_copy(self, off):
            block = self.result(mi, self.mine)
            to = peer(*peer_of(off))
            if self.relayed:
                to = {
                    "slab": lax.rem(slab + lax.rem(off, n_slab), n_slab),
                    "mem": lax.rem(mi + lax.div(off, n_slab), n_mem),
                }
            return remote(block, block, self.sem(2), self.sem(3), to)

        def relay_copy(self, off):
            blocks = self.blocks.at[:, sub]
            to = {"sub": lax.rem(sub + off, n_sub)}
            return remote(blocks, blocks, self.sem(4), self.sem(5), to)

        def relay(self):
            if self.relayed:
                self.arrived(self.span, self.direct, 3)
                each(1, n_sub, lambda off: self.relay_copy(off).start())

        def high_copy(self, off):
            block = self.high.at[self.mine]
            to = self.device(lax.rem(self.index + off, self.size))
            return remote(block, block, self.sem(6), self.sem(7), to)

        def finish(self):
            def body():
                wait_recv(self.target.at[pl.ds(0, self.size - 1)], self.sem(1))
                block = self.result(mi, self.mine)
                if self.size <= 16:
                    value = self.source[self.mine]
                    for off in range(1, self.size):
                        value = value + self.target[lax.rem(self.index + off, self.size)]
                    block[...] = value
                else:
                    block[...] = self.source[self.mine]

                    def add(off):
                        block[...] += self.target[lax.rem(self.index + off, self.size)]

                    each(1, self.size, add)
                if self.high is not None:
                    self.high[self.mine] = block[...].astype(BF16)
                    each(1, self.size, lambda off: self.high_copy(off).start())
                each(1, self.sends + 1, lambda off: self.gather_copy(off).start())

            self.if_owner(body)

        def arrived(self, flat, count, sem):
            self.if_owner(lambda: wait_recv(flat.at[pl.ds(0, count - 1)], self.sem(sem)))
            self.if_owner(lambda: wait_recv(flat.at[pl.ds(0, count)], self.sem(sem)), False)

        def gather(self):
            if self.relayed:
                wait_recv(self.span.at[pl.ds(0, self.handed)], self.sem(5))
            else:
                self.arrived(self.span, self.owners, 3)

        def gather_high(self):
            self.arrived(self.high, self.owners, 7)

        def sent(self):
            self.if_owner(
                lambda: wait_sent(self.source.at[pl.ds(0, self.owners - 1)], self.sem(0))
            )
            self.if_owner(lambda: wait_sent(self.source, self.sem(0)), False)
            self.if_owner(lambda: wait_sent(self.span.at[pl.ds(0, self.sends)], self.sem(2)))
            if self.relayed:
                wait_sent(self.span.at[pl.ds(0, self.handed)], self.sem(4))
            if self.high is not None:
                self.if_owner(
                    lambda: wait_sent(sizes_b.at[pl.ds(0, self.size - 1)], self.sem(6))
                )

    projections = [
        Sum(
            n, me, lambda i: peer(i, mi), part.at[b], rs.at[b],
            lambda mem, o, b=b: ag.at[b, lax.div(mem * owners + o, n_sub), lax.rem(mem * owners + o, n_sub)],
            ag.at[b], x_s, 8 * b, sizes, ag_b if b == 0 else None,
        )
        for b in range(BATCHES)
    ]
    changes = Sum(
        total, mi * n + me, lambda i: peer(lax.rem(i, n), lax.div(i, n)), cpart, crs,
        lambda mem, o: cag.at[o], None, x_s, 14, crs,
    )
    project(0)
    pl.semaphore_wait(barrier, total - 1)
    projections[0].start()
    send_state(0)
    send_state(1)
    project(1)
    projections[1].start()
    projections[0].finish()
    send_state(2)

    def slot(b, s):
        step = owners // n_sub
        return ag[b, s * step : (s + 1) * step].reshape(P_SIZE, own)

    def load_work(columns, extra, b):
        h, m, l = (jnp.concatenate(x, axis=1) for x in zip(*(split3(x) for x in columns)))
        cov = lax.dot_general(
            jnp.concatenate([h, h, m, h, m, l], axis=1),
            jnp.concatenate([h, m, h, l, m, h], axis=1),
            LAST, preferred_element_type=F32,
        )
        r = lax.broadcasted_iota(jnp.int32, (P_SIZE, P_SIZE), 0)
        eye = r == lax.broadcasted_iota(jnp.int32, (P_SIZE, P_SIZE), 1)
        v = var_b[b * P_SIZE : (b + 1) * P_SIZE, :]
        work[:, :P_SIZE] = cov * (1.0 / (M - 1)) + jnp.where(eye, v, 0.0)
        lo = P_SIZE
        for x in extra:
            work[:, lo : lo + own] = x
            lo += own

    def taper(b, at):
        lo = b * P_SIZE
        row = lax.broadcasted_iota(jnp.int32, (P_SIZE, size), 1) + at.start
        c = jnp.concatenate([col_c[lo : lo + P_SIZE, :]] * (size // P_SIZE), axis=1)
        r = jnp.concatenate([col_r[lo : lo + P_SIZE, :]] * (size // P_SIZE), axis=1)
        near = jnp.maximum(1.0 - jnp.abs(row.astype(F32) - c) * r, 0.0)
        return near * near * (1.0 / (M - 1))

    for b in range(BATCHES):
        for c in range(TILES):
            tapers[b, :, tile(c)] = taper(b, tile(c))

    projections[0].gather_high()

    mine_b = ag_b[...].reshape(P_SIZE, own)
    change = 0.0
    for c in range(TILES):
        product = jnp.dot(mine_b, e_all[mi, :, tile(c)], preferred_element_type=F32)
        product = tapers[0, :, tile(c)] * product
        high = product.astype(BF16)
        low = (product - high.astype(F32)).astype(BF16)
        for x in (high, low):
            change = change + lax.dot_general(
                foot[P_SIZE : 2 * P_SIZE, tile(c)], x, LAST, preferred_element_type=F32
            )
    cpart[...] = change.reshape(cpart.shape)
    changes.start()
    projections[1].finish()

    projections[0].relay()
    projections[0].gather()
    first = [slot(0, s) for s in range(n_mem)]
    load_work(first, first, 0)
    root_0 = root_b.at[pl.ds(0, P_SIZE)]
    blocks = P_SIZE // BLOCK
    for k in range(blocks // 2):
        block(work, inv, solved, root_0, k)
        if k == 0:
            send_state(3)
    changes.finish()
    for k in range(blocks // 2, blocks):
        block(work, inv, solved, root_0, k)

    def weights(count):
        h, m, l = split3(solved[:, :count])
        left = jnp.concatenate([h, h, m, h, m, l], axis=0)
        h, m, l = split3(inv[...])
        right = jnp.concatenate([h, m, h, l, m, h], axis=0)
        return lax.dot_general(left, right, FIRST, preferred_element_type=F32).astype(BF16)

    wts[...] = weights(M)
    projections[1].relay()
    first_b = [slot(0, s).astype(BF16) for s in range(n_mem)]

    def cross(b, left, at):
        product = 0.0
        for s in range(n_mem):
            product = product + jnp.dot(left[s], e_all[s, :, at], preferred_element_type=F32)
        tap[:, at] = (tapers[b, :, at] * product).astype(BF16)

    def update(at):
        cross(0, first_b, at)
        for s in range(n_mem):
            moved = jnp.dot(
                wts[s * own : (s + 1) * own, :], tap[:, at], preferred_element_type=F32
            )
            e_all[s, :, at] = (e_all[s, :, at].astype(F32) - moved).astype(BF16)

    for c in range(TILES):
        wait_state(c)
        update(tile(c))

    projections[1].gather()
    changes.gather()
    c_full = jnp.concatenate(split3(cag[...].reshape(P_SIZE, P_SIZE)), axis=0)
    moved = lax.dot_general(c_full, wts[...], LAST, preferred_element_type=F32)
    moved = moved[:P_SIZE] + (moved[P_SIZE : 2 * P_SIZE] + moved[2 * P_SIZE :])
    second = []
    for s in range(n_mem):
        value = slot(1, s) - moved[:, s * own : (s + 1) * own]
        p1[s] = value
        p1_b[s] = value.astype(BF16)
        second.append(value)

    alone = own % P_SIZE == 0
    load_work(second, [p1[mi]] if alone else second, 1)

    used = P_SIZE + (own if alone else M)
    for k in range(blocks):
        block(
            work.at[:, pl.ds(0, used)], inv, solved, root_b.at[pl.ds(P_SIZE, P_SIZE)], k
        )
        cross(1, p1_b, tile(k))
    if alone:
        own_w = weights(own)
    else:
        wts[...] = weights(M)
        own_w = wts[pl.ds(pl.multiple_of(mi * own, own), own), :]

    moved = jnp.dot(own_w, tap[...], preferred_element_type=F32)
    out[...] = (e_all[mi].astype(F32) - moved).astype(BF16)

    wait_sent(e_all.at[pl.ds(0, n_mem - 1)], e_s.at[0])
    for x in projections + [changes]:
        x.sent()


def on_device(shape, state, centers, half_width, radius, order, obs_var):
    n_slab, n_mem, n_sub = shape
    own, rows = state.shape
    n = n_slab * n_sub
    total = n * n_mem
    owners = min(n, 4)
    chunk = P_SIZE // owners
    c_owners = owners * n_mem
    c_chunk = P_SIZE // c_owners
    n_obs = BATCHES * P_SIZE
    operands = (state,) + tuple(
        x[None, :] for x in (centers, half_width, radius, order, obs_var)
    )
    hbm = pl.BlockSpec(memory_space=pltpu.HBM)
    vmem = pl.BlockSpec(memory_space=pltpu.VMEM)
    return pl.pallas_call(
        functools.partial(kernel, shape),
        out_shape=pltpu.VMEM((own, rows), BF16),
        in_specs=[hbm] * 6,
        out_specs=vmem,
        scratch_shapes=[
            pltpu.VMEM((4, 1, n_obs), jnp.int32),
            pltpu.VMEM((1, n_obs), F32),
            pltpu.VMEM((n_mem, own, rows), BF16),
            pltpu.VMEM((n_obs, rows), BF16),
            pltpu.VMEM((P_SIZE, rows), BF16),
            pltpu.VMEM((BATCHES, P_SIZE, rows), F32),
            pltpu.VMEM((n_obs, P_SIZE), F32),
            pltpu.VMEM((n_obs, P_SIZE), F32),
            pltpu.VMEM((n_obs, P_SIZE), F32),
            pltpu.VMEM((n_obs, P_SIZE), F32),
            pltpu.VMEM((P_SIZE, P_SIZE + M), F32),
            pltpu.VMEM((P_SIZE, P_SIZE), F32),
            pltpu.VMEM((P_SIZE, M), F32),
            pltpu.VMEM((M, P_SIZE), BF16),
            pltpu.VMEM((n_mem, P_SIZE, own), F32),
            pltpu.VMEM((n_mem, P_SIZE, own), BF16),
            pltpu.VMEM((BATCHES, owners, chunk, own), F32),
            pltpu.VMEM((BATCHES, n, chunk, own), F32),
            pltpu.VMEM((BATCHES, n_mem * owners // n_sub, n_sub, chunk, own), F32),
            pltpu.VMEM((owners, chunk, own), BF16),
            pltpu.VMEM((c_owners, c_chunk, P_SIZE), F32),
            pltpu.VMEM((total, c_chunk, P_SIZE), F32),
            pltpu.VMEM((c_owners, c_chunk, P_SIZE), F32),
            pltpu.VMEM((total, chunk, own), F32),
            pltpu.VMEM((n, chunk, own), BF16),
            pltpu.SemaphoreType.DMA((3,)),
            pltpu.SemaphoreType.DMA((1 + TILES,)),
            pltpu.SemaphoreType.DMA((18,)),
        ],
        compiler_params=pltpu.CompilerParams(
            collective_id=0, has_side_effects=True, vmem_limit_bytes=40 * 1024 * 1024
        ),
    )(*(pltpu.with_memory_space_constraint(x, pltpu.HBM) for x in operands))


def solution(mesh):
    shape = (mesh.shape["slab"], mesh.shape["mem"], mesh.shape["sub"])
    placed = (P("mem", ("grp", "slab", "sub")), P("grp"), P("grp"), P("grp"), P("grp"), P("grp"))
    return jax.shard_map(
        functools.partial(on_device, shape),
        mesh=mesh,
        in_specs=placed,
        out_specs=P("mem", ("grp", "slab", "sub")),
        check_vma=False,
    )
```

```python
import functools
import math

import jax
import jax.numpy as jnp
from jax import lax
from jax.experimental import pallas as pl
from jax.experimental.pallas import tpu as pltpu
from jax.sharding import PartitionSpec as P

M = 256
P_SIZE = 128
BATCHES = 2
BLOCK = 32
PANEL = 16
TILES = 4

FLOOR = math.exp(-2.0)
F32 = jnp.float32
BF16 = jnp.bfloat16
HIGH = lax.Precision.HIGHEST
LAST = (((1,), (1,)), ((), ()))
FIRST = (((0,), (0,)), ((), ()))


def each(start, stop, body):
    if stop - start <= 16:
        for i in range(start, stop):
            body(i)
    else:

        def step(i, carry):
            body(i)
            return carry

        lax.fori_loop(start, stop, step, 0)


def split3(x):
    high = x.astype(BF16)
    rest = x - high.astype(F32)
    mid = rest.astype(BF16)
    low = (rest - mid.astype(F32)).astype(BF16)
    return high, mid, low


def block(work, inv, solved, root, k):
    b = BLOCK
    size = b // 8
    width = work.shape[1] // P_SIZE
    r0 = k * b

    def at(v):
        return pl.ds(r0 + 8 * v, 8)

    def spread(x, i):
        return jnp.broadcast_to(x[i : i + 1, :], (8, P_SIZE))

    row = lax.broadcasted_iota(jnp.int32, (8, P_SIZE), 0)
    lane = lax.broadcasted_iota(jnp.int32, (8, P_SIZE), 1) - r0
    parts = [
        [work[at(v), g * P_SIZE : (g + 1) * P_SIZE] for v in range(size)] for g in range(width)
    ]
    roots = [root[at(v), :] for v in range(size)]
    pivots = [jnp.ones((8, P_SIZE), F32)] * size
    for j in range(0, b, 2):
        top, jj = j // 8, j % 8
        if j % PANEL == 0:
            cols = {
                i: {
                    v: jnp.broadcast_to(parts[0][v][:, r0 + i : r0 + i + 1], (8, P_SIZE))
                    for v in range(i // 8, size)
                }
                for i in range(j, j + PANEL)
            }
            inside = (lane >= j) & (lane < j + PANEL)
            for v in range(top, size):
                unit = jnp.where(lane == row + 8 * v, 1.0, 0.0) if 8 * v < j + PANEL else 0.0
                parts[0][v] = jnp.where(inside, unit, parts[0][v])
        c0, c1 = cols[j], cols[j + 1]
        p, q, r = spread(c0[top], jj), spread(c0[top], jj + 1), spread(c1[top], jj + 1)
        det = p * r - q * q
        inverse = 1.0 / det
        root_p, root_d = lax.rsqrt(p), lax.rsqrt(det)
        cross = q * root_p
        mix0 = 1.0 / (p * root_p + spread(roots[top], jj))
        mix1 = 1.0 / (det * root_d * root_p + spread(roots[top], jj + 1))
        below = cross * mix0
        after = root_d * root_p * mix1
        ahead = root_p * mix0
        left, right, left_m, right_m = {}, {}, {}, {}
        for v in range(top, size):
            x, y = r * c0[v] - q * c1[v], p * c1[v] - q * c0[v]
            left[v], right[v] = x * inverse, y * inverse
            right_m[v] = y * after
            left_m[v] = c0[v] * ahead - right_m[v] * below
        last = row == jj + 1
        done = row <= jj + 1
        for x, y, z in ((left, right, cross * root_p), (left_m, right_m, below)):
            x[top] = jnp.where(done, jnp.where(last, z, 0.0), x[top])
            y[top] = jnp.where(done, 0.0, y[top])
        pivots[top] = jnp.where(row == jj, p, pivots[top])
        pivots[top] = jnp.where(last, det * root_p * root_p, pivots[top])
        for i in range(j + 2, j - j % PANEL + PANEL):
            s0, s1 = spread(c0[i // 8], i % 8), spread(c1[i // 8], i % 8)
            for v in range(i // 8, size):
                cols[i][v] = cols[i][v] - left[v] * s0 - right[v] * s1
        for g in range(width):
            s0, s1 = spread(parts[g][top], jj), spread(parts[g][top], jj + 1)
            x, y = (left_m, right_m) if g else (left, right)
            for v in range(top, size):
                parts[g][v] = parts[g][v] - x[v] * s0 - y[v] * s1
    for v in range(size):
        scale = lax.rsqrt(pivots[v])
        mixed = 1.0 / (pivots[v] * scale + roots[v])
        for g in range(width):
            parts[g][v] = parts[g][v] * (mixed if g else scale)
        ahead = (lane >= (8 * v // PANEL + 1) * PANEL) & (lane < b)
        parts[0][v] = jnp.where(ahead, 0.0, parts[0][v])
        inv[at(v), :] = jnp.where(lane < b, parts[0][v], 0.0)
        for g in range(1, width):
            solved[at(v), (g - 1) * P_SIZE : g * P_SIZE] = parts[g][v]
    lo = r0 + b
    if lo == P_SIZE:
        return
    pieces = [split3(jnp.concatenate(x, axis=0)) for x in parts]
    h, m, l = pieces[0]
    left = jnp.concatenate([h, h, m, h, m, l], axis=0)
    h, m, l = (jnp.concatenate([x[n] for x in pieces], axis=1) for n in range(3))
    right = jnp.concatenate([h, m, h, l, m, h], axis=0)
    change = lax.dot_general(left, right, FIRST, preferred_element_type=F32)[lo:]
    lane = lax.broadcasted_iota(jnp.int32, (P_SIZE - lo, P_SIZE), 1) - r0
    old = jnp.where((lane >= 0) & (lane < b), 0.0, work[lo:, :P_SIZE])
    work[lo:, :P_SIZE] = old - change[:, :P_SIZE]
    work[lo:, P_SIZE:] -= change[:, P_SIZE:]


def kernel(
    shape,
    state_hbm, cen_hbm, half_hbm, rad_hbm, order_hbm, var_hbm,
    out,
    ints, var,
    e_all, foot, tap, tapers, col_c, col_r, var_b, root_b, work, inv, solved, wts, p1, p1_b,
    part, rs, ag, ag_b, cpart, crs, cag, sizes, sizes_b,
    in_s, e_s, x_s,
):
    n_slab, n_mem, n_sub = shape
    n = n_slab * n_sub
    total = n * n_mem
    own, rows = state_hbm.shape

    mi = lax.axis_index("mem")
    slab, sub = lax.axis_index("slab"), lax.axis_index("sub")
    me = slab * n_sub + sub

    def peer(red, mem):
        return {"slab": lax.div(red, n_sub), "sub": lax.rem(red, n_sub), "mem": mem}

    def peer_of(off):
        red = lax.rem(me + lax.rem(off, n), n)
        mem = lax.rem(mi + lax.div(off, n), n_mem)
        return red, mem

    def remote(src, dst, send, recv, device):
        return pltpu.make_async_remote_copy(
            src_ref=src, dst_ref=dst, send_sem=send, recv_sem=recv,
            device_id=device, device_id_type=pl.DeviceIdType.MESH,
        )

    def wait_sent(ref, sem):
        remote(ref, ref, sem, sem, peer(me, mi)).wait_send()

    def wait_recv(ref, sem):
        remote(ref, ref, sem, sem, peer(me, mi)).wait_recv()

    small = [
        pltpu.make_async_copy(a, ints.at[i], in_s.at[0])
        for i, a in enumerate((cen_hbm, half_hbm, rad_hbm, order_hbm))
    ]
    var_copy = pltpu.make_async_copy(var_hbm, var, in_s.at[1])
    state_copy = pltpu.make_async_copy(state_hbm, e_all.at[mi], in_s.at[2])
    for copy in small:
        copy.start()
    var_copy.start()
    state_copy.start()

    barrier = pltpu.get_barrier_semaphore()

    owners = per = part.shape[1]
    middle = (n - per) // 2
    is_owner = jnp.logical_and(me >= middle, me < middle + per)
    is_other = jnp.logical_not(is_owner)

    def greet(to):
        pl.semaphore_signal(barrier, inc=1, device_id=to, device_id_type=pl.DeviceIdType.MESH)

    @pl.when(is_owner)
    def _():
        each(1, total, lambda off: greet(peer(*peer_of(off))))

    @pl.when(is_other)
    def _():
        each(
            0, per * n_mem,
            lambda o: greet(peer(middle + lax.rem(o, per), lax.rem(mi + lax.div(o, per), n_mem))),
        )
        each(1, n_mem, lambda off: greet({"mem": lax.rem(mi + off, n_mem)}))
        each(1, n_sub, lambda off: greet({"sub": lax.rem(sub + off, n_sub)}))

    pltpu.make_async_copy(ints, ints, in_s.at[0]).wait()
    var_copy.wait()

    n_obs = BATCHES * P_SIZE
    picked = jnp.broadcast_to(ints[3].astype(F32), (P_SIZE, n_obs)).T.astype(jnp.int32)
    lane = lax.broadcasted_iota(jnp.int32, (n_obs, P_SIZE), 1)
    masks = [picked == lane + h * P_SIZE for h in range(BATCHES)]

    def pick(ref):
        value = ref[...].astype(F32)
        chosen = 0.0
        for h in range(BATCHES):
            chosen = chosen + jnp.where(masks[h], value[:, h * P_SIZE : (h + 1) * P_SIZE], 0.0)
        return jnp.sum(chosen, axis=1, keepdims=True)

    center = pick(ints.at[0]) - (me * rows).astype(F32)
    width = pick(ints.at[1])
    variance = pick(var)
    col_c[...] = jnp.broadcast_to(center, (n_obs, P_SIZE))
    col_r[...] = jnp.broadcast_to(1.0 / pick(ints.at[2]), (n_obs, P_SIZE))
    var_b[...] = jnp.broadcast_to(variance, (n_obs, P_SIZE))
    root_b[...] = jnp.broadcast_to(jnp.sqrt(variance), (n_obs, P_SIZE))
    steep = -2.0 / (width * width)
    height = 1.0 / jnp.sqrt(width)

    size = rows // TILES

    def tile(c):
        return pl.ds(c * size, size)

    def e_copy(off, c):
        return remote(
            state_hbm.at[:, tile(c)], e_all.at[mi, :, tile(c)], e_s.at[0], e_s.at[1 + c],
            peer(me, lax.rem(mi + off, n_mem)),
        )

    def send_state(c):
        each(1, n_mem, lambda off: e_copy(off, c).start())

    def wait_state(c):
        wait_recv(e_all.at[pl.ds(0, n_mem - 1), :, tile(c)], e_s.at[1 + c])

    def project(b):
        lo = b * P_SIZE

        def foot_tile(t, carry):
            at = pl.multiple_of(t * 256, 256)
            row = lax.broadcasted_iota(jnp.int32, (P_SIZE, 256), 1) + at
            distance = row.astype(F32) - center[lo : lo + P_SIZE]
            shape_f = jnp.exp(distance * distance * steep[lo : lo + P_SIZE]) - FLOOR
            shape_f = jnp.maximum(shape_f, 0.0) * height[lo : lo + P_SIZE]
            foot[lo : lo + P_SIZE, pl.ds(at, 256)] = shape_f.astype(BF16)
            return carry

        lax.fori_loop(0, rows // 256, foot_tile, 0)
        if b == 0:
            state_copy.wait()
        sums = lax.dot_general(
            foot[lo : lo + P_SIZE, :], e_all[mi], LAST, preferred_element_type=F32
        )
        part[b] = sums.reshape(part.shape[1:])

    class Sum:
        def __init__(self, size, index, device, source, target, result, blocks, sem, base, span, high=None):
            self.size, self.index, self.device = size, index, device
            everyone = blocks is not None
            self.source, self.target, self.result, self.blocks = source, target, result, blocks
            self.everyone = everyone
            self.sems, self.base, self.span, self.high = sem, base, span, high
            self.owners = source.shape[0]
            self.relayed = everyone
            self.mine = lax.rem(me + n * per - middle, per) + (0 if everyone else mi * per)
            self.sends = (n_slab * n_mem if everyone else total) - 1
            self.direct = n_mem * per // n_sub
            self.handed = (n_sub - 1) * self.direct

        def owner_of(self, o):
            return self.device(lax.div(o, per) * n + middle + lax.rem(o, per))

        def sem(self, k):
            return self.sems.at[self.base + k]

        def if_owner(self, body, owner=True):
            pl.when(is_owner if owner else is_other)(body)

        def out_copy(self, off):
            o = lax.rem(self.mine + off, self.owners)
            return remote(
                self.source.at[o], self.target.at[self.index],
                self.sem(0), self.sem(1), self.owner_of(o),
            )

        def start(self):
            each(1, self.owners, lambda off: self.out_copy(off).start())
            self.if_owner(lambda: self.out_copy(0).start(), False)

        def gather_copy(self, off):
            block = self.result(mi, self.mine)
            to = peer(*peer_of(off))
            if self.relayed:
                to = {
                    "slab": lax.rem(slab + lax.rem(off, n_slab), n_slab),
                    "mem": lax.rem(mi + lax.div(off, n_slab), n_mem),
                }
            return remote(block, block, self.sem(2), self.sem(3), to)

        def relay_copy(self, off):
            blocks = self.blocks.at[:, sub]
            to = {"sub": lax.rem(sub + off, n_sub)}
            return remote(blocks, blocks, self.sem(4), self.sem(5), to)

        def relay(self):
            if self.relayed:
                self.arrived(self.span, self.direct, 3)
                each(1, n_sub, lambda off: self.relay_copy(off).start())

        def high_copy(self, off):
            block = self.high.at[self.mine]
            to = self.device(lax.rem(self.index + off, self.size))
            return remote(block, block, self.sem(6), self.sem(7), to)

        def finish(self):
            def body():
                wait_recv(self.target.at[pl.ds(0, self.size - 1)], self.sem(1))
                block = self.result(mi, self.mine)
                if self.size <= 16:
                    value = self.source[self.mine]
                    for off in range(1, self.size):
                        value = value + self.target[lax.rem(self.index + off, self.size)]
                    block[...] = value
                else:
                    block[...] = self.source[self.mine]

                    def add(off):
                        block[...] += self.target[lax.rem(self.index + off, self.size)]

                    each(1, self.size, add)
                if self.high is not None:
                    self.high[self.mine] = block[...].astype(BF16)
                    each(1, self.size, lambda off: self.high_copy(off).start())
                each(1, self.sends + 1, lambda off: self.gather_copy(off).start())

            self.if_owner(body)

        def arrived(self, flat, count, sem):
            self.if_owner(lambda: wait_recv(flat.at[pl.ds(0, count - 1)], self.sem(sem)))
            self.if_owner(lambda: wait_recv(flat.at[pl.ds(0, count)], self.sem(sem)), False)

        def gather(self):
            if self.relayed:
                wait_recv(self.span.at[pl.ds(0, self.handed)], self.sem(5))
            else:
                self.arrived(self.span, self.owners, 3)

        def gather_high(self):
            self.arrived(self.high, self.owners, 7)

        def sent(self):
            self.if_owner(
                lambda: wait_sent(self.source.at[pl.ds(0, self.owners - 1)], self.sem(0))
            )
            self.if_owner(lambda: wait_sent(self.source, self.sem(0)), False)
            self.if_owner(lambda: wait_sent(self.span.at[pl.ds(0, self.sends)], self.sem(2)))
            if self.relayed:
                wait_sent(self.span.at[pl.ds(0, self.handed)], self.sem(4))
            if self.high is not None:
                self.if_owner(
                    lambda: wait_sent(sizes_b.at[pl.ds(0, self.size - 1)], self.sem(6))
                )

    projections = [
        Sum(
            n, me, lambda i: peer(i, mi), part.at[b], rs.at[b],
            lambda mem, o, b=b: ag.at[b, lax.div(mem * owners + o, n_sub), lax.rem(mem * owners + o, n_sub)],
            ag.at[b], x_s, 8 * b, sizes, ag_b if b == 0 else None,
        )
        for b in range(BATCHES)
    ]
    changes = Sum(
        total, mi * n + me, lambda i: peer(lax.rem(i, n), lax.div(i, n)), cpart, crs,
        lambda mem, o: cag.at[o], None, x_s, 14, crs,
    )
    project(0)
    pl.when(is_owner)(lambda: pl.semaphore_wait(barrier, total - 1))
    pl.when(is_other)(lambda: pl.semaphore_wait(barrier, per * n_mem + n_mem + n_sub - 2))
    projections[0].start()
    send_state(0)
    send_state(1)
    project(1)
    projections[1].start()
    projections[0].finish()
    pl.when(is_other)(lambda: send_state(2))

    def slot(b, s):
        step = owners // n_sub
        return ag[b, s * step : (s + 1) * step].reshape(P_SIZE, own)

    def load_work(columns, extra, b):
        h, m, l = (jnp.concatenate(x, axis=1) for x in zip(*(split3(x) for x in columns)))
        cov = lax.dot_general(
            jnp.concatenate([h, h, m, h, m, l], axis=1),
            jnp.concatenate([h, m, h, l, m, h], axis=1),
            LAST, preferred_element_type=F32,
        )
        r = lax.broadcasted_iota(jnp.int32, (P_SIZE, P_SIZE), 0)
        eye = r == lax.broadcasted_iota(jnp.int32, (P_SIZE, P_SIZE), 1)
        v = var_b[b * P_SIZE : (b + 1) * P_SIZE, :]
        work[:, :P_SIZE] = cov * (1.0 / (M - 1)) + jnp.where(eye, v, 0.0)
        lo = P_SIZE
        for x in extra:
            work[:, lo : lo + own] = x
            lo += own

    def taper(b, at):
        lo = b * P_SIZE
        row = lax.broadcasted_iota(jnp.int32, (P_SIZE, size), 1) + at.start
        c = jnp.concatenate([col_c[lo : lo + P_SIZE, :]] * (size // P_SIZE), axis=1)
        r = jnp.concatenate([col_r[lo : lo + P_SIZE, :]] * (size // P_SIZE), axis=1)
        near = jnp.maximum(1.0 - jnp.abs(row.astype(F32) - c) * r, 0.0)
        return near * near * (1.0 / (M - 1))

    for b in range(BATCHES):
        for c in range(TILES):
            tapers[b, :, tile(c)] = taper(b, tile(c))

    projections[1].finish()
    projections[0].gather_high()

    mine_b = ag_b[...].reshape(P_SIZE, own)
    change = 0.0
    for c in range(TILES):
        product = jnp.dot(mine_b, e_all[mi, :, tile(c)], preferred_element_type=F32)
        product = tapers[0, :, tile(c)] * product
        high = product.astype(BF16)
        low = (product - high.astype(F32)).astype(BF16)
        for x in (high, low):
            change = change + lax.dot_general(
                foot[P_SIZE : 2 * P_SIZE, tile(c)], x, LAST, preferred_element_type=F32
            )
    cpart[...] = change.reshape(cpart.shape)
    changes.start()
    pl.when(is_owner)(lambda: send_state(2))
    pl.when(is_other)(lambda: send_state(3))

    projections[0].relay()
    projections[0].gather()
    first = [slot(0, s) for s in range(n_mem)]
    load_work(first, first, 0)
    root_0 = root_b.at[pl.ds(0, P_SIZE)]
    blocks = P_SIZE // BLOCK
    for k in range(blocks // 2):
        block(work, inv, solved, root_0, k)
        if k == 0:
            pl.when(is_owner)(lambda: send_state(3))
    changes.finish()
    for k in range(blocks // 2, blocks):
        block(work, inv, solved, root_0, k)

    def weights(count):
        h, m, l = split3(solved[:, :count])
        left = jnp.concatenate([h, h, m, h, m, l], axis=0)
        h, m, l = split3(inv[...])
        right = jnp.concatenate([h, m, h, l, m, h], axis=0)
        return lax.dot_general(left, right, FIRST, preferred_element_type=F32).astype(BF16)

    wts[...] = weights(M)
    projections[1].relay()
    first_b = [slot(0, s).astype(BF16) for s in range(n_mem)]

    def cross(b, left, at):
        product = 0.0
        for s in range(n_mem):
            product = product + jnp.dot(left[s], e_all[s, :, at], preferred_element_type=F32)
        tap[:, at] = (tapers[b, :, at] * product).astype(BF16)

    def update(at):
        cross(0, first_b, at)
        for s in range(n_mem):
            moved = jnp.dot(
                wts[s * own : (s + 1) * own, :], tap[:, at], preferred_element_type=F32
            )
            e_all[s, :, at] = (e_all[s, :, at].astype(F32) - moved).astype(BF16)

    for c in range(TILES):
        wait_state(c)
        update(tile(c))

    projections[1].gather()
    changes.gather()
    c_full = jnp.concatenate(split3(cag[...].reshape(P_SIZE, P_SIZE)), axis=0)
    moved = lax.dot_general(c_full, wts[...], LAST, preferred_element_type=F32)
    moved = moved[:P_SIZE] + (moved[P_SIZE : 2 * P_SIZE] + moved[2 * P_SIZE :])
    second = []
    for s in range(n_mem):
        value = slot(1, s) - moved[:, s * own : (s + 1) * own]
        p1[s] = value
        p1_b[s] = value.astype(BF16)
        second.append(value)

    alone = own % P_SIZE == 0
    load_work(second, [p1[mi]] if alone else second, 1)

    used = P_SIZE + (own if alone else M)
    for k in range(blocks):
        block(
            work.at[:, pl.ds(0, used)], inv, solved, root_b.at[pl.ds(P_SIZE, P_SIZE)], k
        )
        cross(1, p1_b, tile(k))
    if alone:
        own_w = weights(own)
    else:
        wts[...] = weights(M)
        own_w = wts[pl.ds(pl.multiple_of(mi * own, own), own), :]

    moved = jnp.dot(own_w, tap[...], preferred_element_type=F32)
    out[...] = (e_all[mi].astype(F32) - moved).astype(BF16)

    wait_sent(e_all.at[pl.ds(0, n_mem - 1)], e_s.at[0])
    for x in projections + [changes]:
        x.sent()


def on_device(shape, state, centers, half_width, radius, order, obs_var):
    n_slab, n_mem, n_sub = shape
    own, rows = state.shape
    n = n_slab * n_sub
    total = n * n_mem
    owners = min(n, 4)
    chunk = P_SIZE // owners
    c_owners = owners * n_mem
    c_chunk = P_SIZE // c_owners
    n_obs = BATCHES * P_SIZE
    operands = (state,) + tuple(
        x[None, :] for x in (centers, half_width, radius, order, obs_var)
    )
    hbm = pl.BlockSpec(memory_space=pltpu.HBM)
    vmem = pl.BlockSpec(memory_space=pltpu.VMEM)
    return pl.pallas_call(
        functools.partial(kernel, shape),
        out_shape=pltpu.VMEM((own, rows), BF16),
        in_specs=[hbm] * 6,
        out_specs=vmem,
        scratch_shapes=[
            pltpu.VMEM((4, 1, n_obs), jnp.int32),
            pltpu.VMEM((1, n_obs), F32),
            pltpu.VMEM((n_mem, own, rows), BF16),
            pltpu.VMEM((n_obs, rows), BF16),
            pltpu.VMEM((P_SIZE, rows), BF16),
            pltpu.VMEM((BATCHES, P_SIZE, rows), F32),
            pltpu.VMEM((n_obs, P_SIZE), F32),
            pltpu.VMEM((n_obs, P_SIZE), F32),
            pltpu.VMEM((n_obs, P_SIZE), F32),
            pltpu.VMEM((n_obs, P_SIZE), F32),
            pltpu.VMEM((P_SIZE, P_SIZE + M), F32),
            pltpu.VMEM((P_SIZE, P_SIZE), F32),
            pltpu.VMEM((P_SIZE, M), F32),
            pltpu.VMEM((M, P_SIZE), BF16),
            pltpu.VMEM((n_mem, P_SIZE, own), F32),
            pltpu.VMEM((n_mem, P_SIZE, own), BF16),
            pltpu.VMEM((BATCHES, owners, chunk, own), F32),
            pltpu.VMEM((BATCHES, n, chunk, own), F32),
            pltpu.VMEM((BATCHES, n_mem * owners // n_sub, n_sub, chunk, own), F32),
            pltpu.VMEM((owners, chunk, own), BF16),
            pltpu.VMEM((c_owners, c_chunk, P_SIZE), F32),
            pltpu.VMEM((total, c_chunk, P_SIZE), F32),
            pltpu.VMEM((c_owners, c_chunk, P_SIZE), F32),
            pltpu.VMEM((total, chunk, own), F32),
            pltpu.VMEM((n, chunk, own), BF16),
            pltpu.SemaphoreType.DMA((3,)),
            pltpu.SemaphoreType.DMA((1 + TILES,)),
            pltpu.SemaphoreType.DMA((18,)),
        ],
        compiler_params=pltpu.CompilerParams(
            collective_id=0, has_side_effects=True, vmem_limit_bytes=40 * 1024 * 1024
        ),
    )(*(pltpu.with_memory_space_constraint(x, pltpu.HBM) for x in operands))


def solution(mesh):
    shape = (mesh.shape["slab"], mesh.shape["mem"], mesh.shape["sub"])
    placed = (P("mem", ("grp", "slab", "sub")), P("grp"), P("grp"), P("grp"), P("grp"), P("grp"))
    return jax.shard_map(
        functools.partial(on_device, shape),
        mesh=mesh,
        in_specs=placed,
        out_specs=P("mem", ("grp", "slab", "sub")),
        check_vma=False,
    )
```

```python
import functools
import math

import jax
import jax.numpy as jnp
from jax import lax
from jax.experimental import pallas as pl
from jax.experimental.pallas import tpu as pltpu
from jax.sharding import PartitionSpec as P

M = 256
P_SIZE = 128
BATCHES = 2
BLOCK = 32
PANEL = 16
TILES = 4

FLOOR = math.exp(-2.0)
F32 = jnp.float32
BF16 = jnp.bfloat16
HIGH = lax.Precision.HIGHEST
LAST = (((1,), (1,)), ((), ()))
FIRST = (((0,), (0,)), ((), ()))


def each(start, stop, body):
    if stop - start <= 16:
        for i in range(start, stop):
            body(i)
    else:

        def step(i, carry):
            body(i)
            return carry

        lax.fori_loop(start, stop, step, 0)


def split3(x):
    high = x.astype(BF16)
    rest = x - high.astype(F32)
    mid = rest.astype(BF16)
    low = (rest - mid.astype(F32)).astype(BF16)
    return high, mid, low


def block(work, inv, solved, root, k):
    b = BLOCK
    size = b // 8
    width = work.shape[1] // P_SIZE
    r0 = k * b

    def at(v):
        return pl.ds(r0 + 8 * v, 8)

    def spread(x, i):
        return jnp.broadcast_to(x[i : i + 1, :], (8, P_SIZE))

    row = lax.broadcasted_iota(jnp.int32, (8, P_SIZE), 0)
    lane = lax.broadcasted_iota(jnp.int32, (8, P_SIZE), 1) - r0
    parts = [
        [work[at(v), g * P_SIZE : (g + 1) * P_SIZE] for v in range(size)] for g in range(width)
    ]
    roots = [root[at(v), :] for v in range(size)]
    pivots = [jnp.ones((8, P_SIZE), F32)] * size
    for j in range(0, b, 2):
        top, jj = j // 8, j % 8
        if j % PANEL == 0:
            cols = {
                i: {
                    v: jnp.broadcast_to(parts[0][v][:, r0 + i : r0 + i + 1], (8, P_SIZE))
                    for v in range(i // 8, size)
                }
                for i in range(j, j + PANEL)
            }
            inside = (lane >= j) & (lane < j + PANEL)
            for v in range(top, size):
                unit = jnp.where(lane == row + 8 * v, 1.0, 0.0) if 8 * v < j + PANEL else 0.0
                parts[0][v] = jnp.where(inside, unit, parts[0][v])
        c0, c1 = cols[j], cols[j + 1]
        p, q, r = spread(c0[top], jj), spread(c0[top], jj + 1), spread(c1[top], jj + 1)
        det = p * r - q * q
        inverse = 1.0 / det
        root_p, root_d = lax.rsqrt(p), lax.rsqrt(det)
        cross = q * root_p
        mix0 = 1.0 / (p * root_p + spread(roots[top], jj))
        mix1 = 1.0 / (det * root_d * root_p + spread(roots[top], jj + 1))
        below = cross * mix0
        after = root_d * root_p * mix1
        ahead = root_p * mix0
        left, right, left_m, right_m = {}, {}, {}, {}
        for v in range(top, size):
            x, y = r * c0[v] - q * c1[v], p * c1[v] - q * c0[v]
            left[v], right[v] = x * inverse, y * inverse
            right_m[v] = y * after
            left_m[v] = c0[v] * ahead - right_m[v] * below
        last = row == jj + 1
        done = row <= jj + 1
        for x, y, z in ((left, right, cross * root_p), (left_m, right_m, below)):
            x[top] = jnp.where(done, jnp.where(last, z, 0.0), x[top])
            y[top] = jnp.where(done, 0.0, y[top])
        pivots[top] = jnp.where(row == jj, p, pivots[top])
        pivots[top] = jnp.where(last, det * root_p * root_p, pivots[top])
        for i in range(j + 2, j - j % PANEL + PANEL):
            s0, s1 = spread(c0[i // 8], i % 8), spread(c1[i // 8], i % 8)
            for v in range(i // 8, size):
                cols[i][v] = cols[i][v] - left[v] * s0 - right[v] * s1
        for g in range(width):
            s0, s1 = spread(parts[g][top], jj), spread(parts[g][top], jj + 1)
            x, y = (left_m, right_m) if g else (left, right)
            for v in range(top, size):
                parts[g][v] = parts[g][v] - x[v] * s0 - y[v] * s1
    for v in range(size):
        scale = lax.rsqrt(pivots[v])
        mixed = 1.0 / (pivots[v] * scale + roots[v])
        for g in range(width):
            parts[g][v] = parts[g][v] * (mixed if g else scale)
        ahead = (lane >= (8 * v // PANEL + 1) * PANEL) & (lane < b)
        parts[0][v] = jnp.where(ahead, 0.0, parts[0][v])
        inv[at(v), :] = jnp.where(lane < b, parts[0][v], 0.0)
        for g in range(1, width):
            solved[at(v), (g - 1) * P_SIZE : g * P_SIZE] = parts[g][v]
    lo = r0 + b
    if lo == P_SIZE:
        return
    pieces = [split3(jnp.concatenate(x, axis=0)) for x in parts]
    h, m, l = pieces[0]
    left = jnp.concatenate([h, h, m, h, m, l], axis=0)
    h, m, l = (jnp.concatenate([x[n] for x in pieces], axis=1) for n in range(3))
    right = jnp.concatenate([h, m, h, l, m, h], axis=0)
    change = lax.dot_general(left, right, FIRST, preferred_element_type=F32)[lo:]
    lane = lax.broadcasted_iota(jnp.int32, (P_SIZE - lo, P_SIZE), 1) - r0
    old = jnp.where((lane >= 0) & (lane < b), 0.0, work[lo:, :P_SIZE])
    work[lo:, :P_SIZE] = old - change[:, :P_SIZE]
    work[lo:, P_SIZE:] -= change[:, P_SIZE:]


def kernel(
    shape,
    state_hbm, cen_hbm, half_hbm, rad_hbm, order_hbm, var_hbm,
    out,
    ints, var,
    e_all, foot, tap, tapers, col_c, col_r, var_b, root_b, work, inv, solved, wts, p1, p1_b,
    part, rs, ag, ag_b, cpart, crs, cag, sizes, sizes_b,
    in_s, e_s, x_s,
):
    n_slab, n_mem, n_sub = shape
    n = n_slab * n_sub
    total = n * n_mem
    own, rows = state_hbm.shape

    mi = lax.axis_index("mem")
    slab, sub = lax.axis_index("slab"), lax.axis_index("sub")
    me = slab * n_sub + sub

    def peer(red, mem):
        return {"slab": lax.div(red, n_sub), "sub": lax.rem(red, n_sub), "mem": mem}

    def peer_of(off):
        red = lax.rem(me + lax.rem(off, n), n)
        mem = lax.rem(mi + lax.div(off, n), n_mem)
        return red, mem

    def remote(src, dst, send, recv, device):
        return pltpu.make_async_remote_copy(
            src_ref=src, dst_ref=dst, send_sem=send, recv_sem=recv,
            device_id=device, device_id_type=pl.DeviceIdType.MESH,
        )

    def wait_sent(ref, sem):
        remote(ref, ref, sem, sem, peer(me, mi)).wait_send()

    def wait_recv(ref, sem):
        remote(ref, ref, sem, sem, peer(me, mi)).wait_recv()

    small = [
        pltpu.make_async_copy(a, ints.at[i], in_s.at[0])
        for i, a in enumerate((cen_hbm, half_hbm, rad_hbm, order_hbm))
    ]
    var_copy = pltpu.make_async_copy(var_hbm, var, in_s.at[1])
    state_copy = pltpu.make_async_copy(state_hbm, e_all.at[mi], in_s.at[2])
    for copy in small:
        copy.start()
    var_copy.start()
    state_copy.start()

    barrier = pltpu.get_barrier_semaphore()

    owners = per = part.shape[1]
    middle = (n - per) // 2
    is_owner = jnp.logical_and(me >= middle, me < middle + per)
    is_other = jnp.logical_not(is_owner)

    def greet(to):
        pl.semaphore_signal(barrier, inc=1, device_id=to, device_id_type=pl.DeviceIdType.MESH)

    @pl.when(is_owner)
    def _():
        each(1, total, lambda off: greet(peer(*peer_of(off))))

    @pl.when(is_other)
    def _():
        each(
            0, per * n_mem,
            lambda o: greet(peer(middle + lax.rem(o, per), lax.rem(mi + lax.div(o, per), n_mem))),
        )
        each(1, n_mem, lambda off: greet({"mem": lax.rem(mi + off, n_mem)}))
        each(1, n_sub, lambda off: greet({"sub": lax.rem(sub + off, n_sub)}))

    pltpu.make_async_copy(ints, ints, in_s.at[0]).wait()
    var_copy.wait()

    n_obs = BATCHES * P_SIZE
    picked = jnp.broadcast_to(ints[3].astype(F32), (P_SIZE, n_obs)).T.astype(jnp.int32)
    lane = lax.broadcasted_iota(jnp.int32, (n_obs, P_SIZE), 1)
    masks = [picked == lane + h * P_SIZE for h in range(BATCHES)]

    def pick(ref):
        value = ref[...].astype(F32)
        chosen = 0.0
        for h in range(BATCHES):
            chosen = chosen + jnp.where(masks[h], value[:, h * P_SIZE : (h + 1) * P_SIZE], 0.0)
        return jnp.sum(chosen, axis=1, keepdims=True)

    center = pick(ints.at[0]) - (me * rows).astype(F32)
    width = pick(ints.at[1])
    variance = pick(var)
    col_c[...] = jnp.broadcast_to(center, (n_obs, P_SIZE))
    col_r[...] = jnp.broadcast_to(1.0 / pick(ints.at[2]), (n_obs, P_SIZE))
    var_b[...] = jnp.broadcast_to(variance, (n_obs, P_SIZE))
    root_b[...] = jnp.broadcast_to(jnp.sqrt(variance), (n_obs, P_SIZE))
    steep = -2.0 / (width * width)
    height = 1.0 / jnp.sqrt(width)

    size = rows // TILES

    def tile(c):
        return pl.ds(c * size, size)

    def e_copy(off, c):
        return remote(
            state_hbm.at[:, tile(c)], e_all.at[mi, :, tile(c)], e_s.at[0], e_s.at[1 + c],
            peer(me, lax.rem(mi + off, n_mem)),
        )

    def send_state(c):
        each(1, n_mem, lambda off: e_copy(off, c).start())

    def wait_state(c):
        wait_recv(e_all.at[pl.ds(0, n_mem - 1), :, tile(c)], e_s.at[1 + c])

    def project(b):
        lo = b * P_SIZE

        def foot_tile(t, carry):
            at = pl.multiple_of(t * 256, 256)
            row = lax.broadcasted_iota(jnp.int32, (P_SIZE, 256), 1) + at
            distance = row.astype(F32) - center[lo : lo + P_SIZE]
            shape_f = jnp.exp(distance * distance * steep[lo : lo + P_SIZE]) - FLOOR
            shape_f = jnp.maximum(shape_f, 0.0) * height[lo : lo + P_SIZE]
            foot[lo : lo + P_SIZE, pl.ds(at, 256)] = shape_f.astype(BF16)
            return carry

        lax.fori_loop(0, rows // 256, foot_tile, 0)
        if b == 0:
            state_copy.wait()
        sums = lax.dot_general(
            foot[lo : lo + P_SIZE, :], e_all[mi], LAST, preferred_element_type=F32
        )
        part[b] = sums.reshape(part.shape[1:])

    class Sum:
        def __init__(self, size, index, device, source, target, result, blocks, sem, base, span, high=None):
            self.size, self.index, self.device = size, index, device
            everyone = blocks is not None
            self.source, self.target, self.result, self.blocks = source, target, result, blocks
            self.everyone = everyone
            self.sems, self.base, self.span, self.high = sem, base, span, high
            self.owners = source.shape[0]
            self.relayed = everyone
            self.mine = lax.rem(me + n * per - middle, per) + (0 if everyone else mi * per)
            self.sends = (n_slab * n_mem if everyone else total) - 1
            self.direct = n_mem * per // n_sub
            self.handed = (n_sub - 1) * self.direct

        def owner_of(self, o):
            return self.device(lax.div(o, per) * n + middle + lax.rem(o, per))

        def sem(self, k):
            return self.sems.at[self.base + k]

        def if_owner(self, body, owner=True):
            pl.when(is_owner if owner else is_other)(body)

        def out_copy(self, off):
            o = lax.rem(self.mine + off, self.owners)
            return remote(
                self.source.at[o], self.target.at[self.index],
                self.sem(0), self.sem(1), self.owner_of(o),
            )

        def start(self):
            each(1, self.owners, lambda off: self.out_copy(off).start())
            self.if_owner(lambda: self.out_copy(0).start(), False)

        def start_side(self, q, last):
            def copy(off):
                o = q * per + lax.rem(me + n * per - middle + off, per)
                return remote(
                    self.source.at[o], self.target.at[self.index],
                    self.sem(0), self.sem(1), self.owner_of(o),
                )

            each(1 if last else 0, per, lambda off: copy(off).start())
            if last:
                self.if_owner(lambda: copy(0).start(), False)

        def gather_copy(self, off):
            block = self.result(mi, self.mine)
            to = peer(*peer_of(off))
            if self.relayed:
                to = {
                    "slab": lax.rem(slab + lax.rem(off, n_slab), n_slab),
                    "mem": lax.rem(mi + lax.div(off, n_slab), n_mem),
                }
            return remote(block, block, self.sem(2), self.sem(3), to)

        def relay_copy(self, off):
            blocks = self.blocks.at[:, sub]
            to = {"sub": lax.rem(sub + off, n_sub)}
            return remote(blocks, blocks, self.sem(4), self.sem(5), to)

        def relay(self):
            if self.relayed:
                self.arrived(self.span, self.direct, 3)
                each(1, n_sub, lambda off: self.relay_copy(off).start())

        def high_copy(self, off):
            block = self.high.at[self.mine]
            to = self.device(lax.rem(self.index + off, self.size))
            return remote(block, block, self.sem(6), self.sem(7), to)

        def finish(self):
            def body():
                wait_recv(self.target.at[pl.ds(0, self.size - 1)], self.sem(1))
                block = self.result(mi, self.mine)
                if self.size <= 16:
                    value = self.source[self.mine]
                    for off in range(1, self.size):
                        value = value + self.target[lax.rem(self.index + off, self.size)]
                    block[...] = value
                else:
                    block[...] = self.source[self.mine]

                    def add(off):
                        block[...] += self.target[lax.rem(self.index + off, self.size)]

                    each(1, self.size, add)
                if self.high is not None:
                    self.high[self.mine] = block[...].astype(BF16)
                    each(1, self.size, lambda off: self.high_copy(off).start())
                turn = (lambda off: off) if self.relayed else (lambda off: total - off)
                each(1, self.sends + 1, lambda off: self.gather_copy(turn(off)).start())

            self.if_owner(body)

        def arrived(self, flat, count, sem):
            self.if_owner(lambda: wait_recv(flat.at[pl.ds(0, count - 1)], self.sem(sem)))
            self.if_owner(lambda: wait_recv(flat.at[pl.ds(0, count)], self.sem(sem)), False)

        def gather(self):
            if self.relayed:
                wait_recv(self.span.at[pl.ds(0, self.handed)], self.sem(5))
            else:
                self.arrived(self.span, self.owners, 3)

        def gather_high(self):
            self.arrived(self.high, self.owners, 7)

        def sent(self):
            self.if_owner(
                lambda: wait_sent(self.source.at[pl.ds(0, self.owners - 1)], self.sem(0))
            )
            self.if_owner(lambda: wait_sent(self.source, self.sem(0)), False)
            self.if_owner(lambda: wait_sent(self.span.at[pl.ds(0, self.sends)], self.sem(2)))
            if self.relayed:
                wait_sent(self.span.at[pl.ds(0, self.handed)], self.sem(4))
            if self.high is not None:
                self.if_owner(
                    lambda: wait_sent(sizes_b.at[pl.ds(0, self.size - 1)], self.sem(6))
                )

    projections = [
        Sum(
            n, me, lambda i: peer(i, mi), part.at[b], rs.at[b],
            lambda mem, o, b=b: ag.at[b, lax.div(mem * owners + o, n_sub), lax.rem(mem * owners + o, n_sub)],
            ag.at[b], x_s, 8 * b, sizes, ag_b if b == 0 else None,
        )
        for b in range(BATCHES)
    ]
    changes = Sum(
        total, mi * n + me, lambda i: peer(lax.rem(i, n), lax.div(i, n)), cpart, crs,
        lambda mem, o: cag.at[o], None, x_s, 14, crs,
    )
    project(0)
    pl.when(is_owner)(lambda: pl.semaphore_wait(barrier, total - 1))
    pl.when(is_other)(lambda: pl.semaphore_wait(barrier, per * n_mem + n_mem + n_sub - 2))
    projections[0].start()
    send_state(0)
    send_state(1)
    project(1)
    projections[1].start()
    projections[0].finish()
    pl.when(is_other)(lambda: send_state(2))

    def slot(b, s):
        step = owners // n_sub
        return ag[b, s * step : (s + 1) * step].reshape(P_SIZE, own)

    def load_work(columns, extra, b):
        h, m, l = (jnp.concatenate(x, axis=1) for x in zip(*(split3(x) for x in columns)))
        cov = lax.dot_general(
            jnp.concatenate([h, h, m, h, m, l], axis=1),
            jnp.concatenate([h, m, h, l, m, h], axis=1),
            LAST, preferred_element_type=F32,
        )
        r = lax.broadcasted_iota(jnp.int32, (P_SIZE, P_SIZE), 0)
        eye = r == lax.broadcasted_iota(jnp.int32, (P_SIZE, P_SIZE), 1)
        v = var_b[b * P_SIZE : (b + 1) * P_SIZE, :]
        work[:, :P_SIZE] = cov * (1.0 / (M - 1)) + jnp.where(eye, v, 0.0)
        lo = P_SIZE
        for x in extra:
            work[:, lo : lo + own] = x
            lo += own

    def taper(b, at):
        lo = b * P_SIZE
        row = lax.broadcasted_iota(jnp.int32, (P_SIZE, size), 1) + at.start
        c = jnp.concatenate([col_c[lo : lo + P_SIZE, :]] * (size // P_SIZE), axis=1)
        r = jnp.concatenate([col_r[lo : lo + P_SIZE, :]] * (size // P_SIZE), axis=1)
        near = jnp.maximum(1.0 - jnp.abs(row.astype(F32) - c) * r, 0.0)
        return near * near * (1.0 / (M - 1))

    for b in range(BATCHES):
        for c in range(TILES):
            tapers[b, :, tile(c)] = taper(b, tile(c))

    projections[1].finish()
    projections[0].gather_high()

    side, step = P_SIZE // n_mem, per // n_mem
    for k in range(1, n_mem + 1):
        q = lax.rem(mi + k, n_mem)
        at = pl.ds(pl.multiple_of(q * side, side), side)
        left = ag_b[pl.ds(q * step, step)].reshape(side, own)
        change = 0.0
        for c in range(TILES):
            product = jnp.dot(left, e_all[mi, :, tile(c)], preferred_element_type=F32)
            product = tapers[0, at, tile(c)] * product
            high = product.astype(BF16)
            low = (product - high.astype(F32)).astype(BF16)
            change = change + lax.dot_general(
                jnp.concatenate([high, low], axis=0), foot[P_SIZE : 2 * P_SIZE, tile(c)],
                LAST, preferred_element_type=F32,
            )
        change = change[:side] + change[side:]
        cpart[pl.ds(q * per, per)] = change.reshape(per, cpart.shape[1], P_SIZE)
        changes.start_side(q, k == n_mem)
    pl.when(is_owner)(lambda: send_state(2))
    pl.when(is_other)(lambda: send_state(3))

    projections[0].relay()
    projections[0].gather()
    first = [slot(0, s) for s in range(n_mem)]
    load_work(first, first, 0)
    root_0 = root_b.at[pl.ds(0, P_SIZE)]
    blocks = P_SIZE // BLOCK
    for k in range(blocks // 2):
        block(work, inv, solved, root_0, k)
        if k == 0:
            pl.when(is_owner)(lambda: send_state(3))
    changes.finish()
    for k in range(blocks // 2, blocks):
        block(work, inv, solved, root_0, k)

    def weights(count):
        h, m, l = split3(solved[:, :count])
        left = jnp.concatenate([h, h, m, h, m, l], axis=0)
        h, m, l = split3(inv[...])
        right = jnp.concatenate([h, m, h, l, m, h], axis=0)
        return lax.dot_general(left, right, FIRST, preferred_element_type=F32).astype(BF16)

    wts[...] = weights(M)
    projections[1].relay()
    first_b = [slot(0, s).astype(BF16) for s in range(n_mem)]

    def cross(b, left, at):
        product = 0.0
        for s in range(n_mem):
            product = product + jnp.dot(left[s], e_all[s, :, at], preferred_element_type=F32)
        tap[:, at] = (tapers[b, :, at] * product).astype(BF16)

    def update(at):
        cross(0, first_b, at)
        for s in range(n_mem):
            moved = jnp.dot(
                wts[s * own : (s + 1) * own, :], tap[:, at], preferred_element_type=F32
            )
            e_all[s, :, at] = (e_all[s, :, at].astype(F32) - moved).astype(BF16)

    for c in range(TILES):
        wait_state(c)
        update(tile(c))

    projections[1].gather()
    changes.gather()
    c_full = jnp.concatenate(split3(cag[...].reshape(P_SIZE, P_SIZE).T), axis=0)
    moved = lax.dot_general(c_full, wts[...], LAST, preferred_element_type=F32)
    moved = moved[:P_SIZE] + (moved[P_SIZE : 2 * P_SIZE] + moved[2 * P_SIZE :])
    second = []
    for s in range(n_mem):
        value = slot(1, s) - moved[:, s * own : (s + 1) * own]
        p1[s] = value
        p1_b[s] = value.astype(BF16)
        second.append(value)

    alone = own % P_SIZE == 0
    load_work(second, [p1[mi]] if alone else second, 1)

    used = P_SIZE + (own if alone else M)
    for k in range(blocks):
        block(
            work.at[:, pl.ds(0, used)], inv, solved, root_b.at[pl.ds(P_SIZE, P_SIZE)], k
        )
        cross(1, p1_b, tile(k))
    if alone:
        own_w = weights(own)
    else:
        wts[...] = weights(M)
        own_w = wts[pl.ds(pl.multiple_of(mi * own, own), own), :]

    moved = jnp.dot(own_w, tap[...], preferred_element_type=F32)
    out[...] = (e_all[mi].astype(F32) - moved).astype(BF16)

    wait_sent(e_all.at[pl.ds(0, n_mem - 1)], e_s.at[0])
    for x in projections + [changes]:
        x.sent()


def on_device(shape, state, centers, half_width, radius, order, obs_var):
    n_slab, n_mem, n_sub = shape
    own, rows = state.shape
    n = n_slab * n_sub
    total = n * n_mem
    owners = min(n, 4)
    chunk = P_SIZE // owners
    c_owners = owners * n_mem
    c_chunk = P_SIZE // c_owners
    n_obs = BATCHES * P_SIZE
    operands = (state,) + tuple(
        x[None, :] for x in (centers, half_width, radius, order, obs_var)
    )
    hbm = pl.BlockSpec(memory_space=pltpu.HBM)
    vmem = pl.BlockSpec(memory_space=pltpu.VMEM)
    return pl.pallas_call(
        functools.partial(kernel, shape),
        out_shape=pltpu.VMEM((own, rows), BF16),
        in_specs=[hbm] * 6,
        out_specs=vmem,
        scratch_shapes=[
            pltpu.VMEM((4, 1, n_obs), jnp.int32),
            pltpu.VMEM((1, n_obs), F32),
            pltpu.VMEM((n_mem, own, rows), BF16),
            pltpu.VMEM((n_obs, rows), BF16),
            pltpu.VMEM((P_SIZE, rows), BF16),
            pltpu.VMEM((BATCHES, P_SIZE, rows), F32),
            pltpu.VMEM((n_obs, P_SIZE), F32),
            pltpu.VMEM((n_obs, P_SIZE), F32),
            pltpu.VMEM((n_obs, P_SIZE), F32),
            pltpu.VMEM((n_obs, P_SIZE), F32),
            pltpu.VMEM((P_SIZE, P_SIZE + M), F32),
            pltpu.VMEM((P_SIZE, P_SIZE), F32),
            pltpu.VMEM((P_SIZE, M), F32),
            pltpu.VMEM((M, P_SIZE), BF16),
            pltpu.VMEM((n_mem, P_SIZE, own), F32),
            pltpu.VMEM((n_mem, P_SIZE, own), BF16),
            pltpu.VMEM((BATCHES, owners, chunk, own), F32),
            pltpu.VMEM((BATCHES, n, chunk, own), F32),
            pltpu.VMEM((BATCHES, n_mem * owners // n_sub, n_sub, chunk, own), F32),
            pltpu.VMEM((owners, chunk, own), BF16),
            pltpu.VMEM((c_owners, c_chunk, P_SIZE), F32),
            pltpu.VMEM((total, c_chunk, P_SIZE), F32),
            pltpu.VMEM((c_owners, c_chunk, P_SIZE), F32),
            pltpu.VMEM((total, chunk, own), F32),
            pltpu.VMEM((n, chunk, own), BF16),
            pltpu.SemaphoreType.DMA((3,)),
            pltpu.SemaphoreType.DMA((1 + TILES,)),
            pltpu.SemaphoreType.DMA((18,)),
        ],
        compiler_params=pltpu.CompilerParams(
            collective_id=0, has_side_effects=True, vmem_limit_bytes=40 * 1024 * 1024
        ),
    )(*(pltpu.with_memory_space_constraint(x, pltpu.HBM) for x in operands))


def solution(mesh):
    shape = (mesh.shape["slab"], mesh.shape["mem"], mesh.shape["sub"])
    placed = (P("mem", ("grp", "slab", "sub")), P("grp"), P("grp"), P("grp"), P("grp"), P("grp"))
    return jax.shard_map(
        functools.partial(on_device, shape),
        mesh=mesh,
        in_specs=placed,
        out_specs=P("mem", ("grp", "slab", "sub")),
        check_vma=False,
    )
```

```python
import functools
import math

import jax
import jax.numpy as jnp
from jax import lax
from jax.experimental import pallas as pl
from jax.experimental.pallas import tpu as pltpu
from jax.sharding import PartitionSpec as P

M = 256
P_SIZE = 128
BATCHES = 2
BLOCK = 32
PANEL = 16
TILES = 4

FLOOR = math.exp(-2.0)
F32 = jnp.float32
BF16 = jnp.bfloat16
HIGH = lax.Precision.HIGHEST
LAST = (((1,), (1,)), ((), ()))
FIRST = (((0,), (0,)), ((), ()))


def each(start, stop, body):
    if stop - start <= 16:
        for i in range(start, stop):
            body(i)
    else:

        def step(i, carry):
            body(i)
            return carry

        lax.fori_loop(start, stop, step, 0)


def split3(x):
    high = x.astype(BF16)
    rest = x - high.astype(F32)
    mid = rest.astype(BF16)
    low = (rest - mid.astype(F32)).astype(BF16)
    return high, mid, low


def block(work, inv, solved, root, k):
    b = BLOCK
    size = b // 8
    width = work.shape[1] // P_SIZE
    r0 = k * b

    def at(v):
        return pl.ds(r0 + 8 * v, 8)

    def spread(x, i):
        return jnp.broadcast_to(x[i : i + 1, :], (8, P_SIZE))

    row = lax.broadcasted_iota(jnp.int32, (8, P_SIZE), 0)
    lane = lax.broadcasted_iota(jnp.int32, (8, P_SIZE), 1) - r0
    parts = [
        [work[at(v), g * P_SIZE : (g + 1) * P_SIZE] for v in range(size)] for g in range(width)
    ]
    roots = [root[at(v), :] for v in range(size)]
    pivots = [jnp.ones((8, P_SIZE), F32)] * size
    for j in range(0, b, 2):
        top, jj = j // 8, j % 8
        if j % PANEL == 0:
            cols = {
                i: {
                    v: jnp.broadcast_to(parts[0][v][:, r0 + i : r0 + i + 1], (8, P_SIZE))
                    for v in range(i // 8, size)
                }
                for i in range(j, j + PANEL)
            }
            inside = (lane >= j) & (lane < j + PANEL)
            for v in range(top, size):
                unit = jnp.where(lane == row + 8 * v, 1.0, 0.0) if 8 * v < j + PANEL else 0.0
                parts[0][v] = jnp.where(inside, unit, parts[0][v])
        c0, c1 = cols[j], cols[j + 1]
        p, q, r = spread(c0[top], jj), spread(c0[top], jj + 1), spread(c1[top], jj + 1)
        det = p * r - q * q
        inverse = 1.0 / det
        root_p, root_d = lax.rsqrt(p), lax.rsqrt(det)
        cross = q * root_p
        mix0 = 1.0 / (p * root_p + spread(roots[top], jj))
        mix1 = 1.0 / (det * root_d * root_p + spread(roots[top], jj + 1))
        below = cross * mix0
        after = root_d * root_p * mix1
        ahead = root_p * mix0
        left, right, left_m, right_m = {}, {}, {}, {}
        for v in range(top, size):
            x, y = r * c0[v] - q * c1[v], p * c1[v] - q * c0[v]
            left[v], right[v] = x * inverse, y * inverse
            right_m[v] = y * after
            left_m[v] = c0[v] * ahead - right_m[v] * below
        last = row == jj + 1
        done = row <= jj + 1
        for x, y, z in ((left, right, cross * root_p), (left_m, right_m, below)):
            x[top] = jnp.where(done, jnp.where(last, z, 0.0), x[top])
            y[top] = jnp.where(done, 0.0, y[top])
        pivots[top] = jnp.where(row == jj, p, pivots[top])
        pivots[top] = jnp.where(last, det * root_p * root_p, pivots[top])
        for i in range(j + 2, j - j % PANEL + PANEL):
            s0, s1 = spread(c0[i // 8], i % 8), spread(c1[i // 8], i % 8)
            for v in range(i // 8, size):
                cols[i][v] = cols[i][v] - left[v] * s0 - right[v] * s1
        for g in range(width):
            s0, s1 = spread(parts[g][top], jj), spread(parts[g][top], jj + 1)
            x, y = (left_m, right_m) if g else (left, right)
            for v in range(top, size):
                parts[g][v] = parts[g][v] - x[v] * s0 - y[v] * s1
    for v in range(size):
        scale = lax.rsqrt(pivots[v])
        mixed = 1.0 / (pivots[v] * scale + roots[v])
        for g in range(width):
            parts[g][v] = parts[g][v] * (mixed if g else scale)
        ahead = (lane >= (8 * v // PANEL + 1) * PANEL) & (lane < b)
        parts[0][v] = jnp.where(ahead, 0.0, parts[0][v])
        inv[at(v), :] = jnp.where(lane < b, parts[0][v], 0.0)
        for g in range(1, width):
            solved[at(v), (g - 1) * P_SIZE : g * P_SIZE] = parts[g][v]
    lo = r0 + b
    if lo == P_SIZE:
        return
    pieces = [split3(jnp.concatenate(x, axis=0)) for x in parts]
    h, m, l = pieces[0]
    left = jnp.concatenate([h, h, m, h, m, l], axis=0)
    h, m, l = (jnp.concatenate([x[n] for x in pieces], axis=1) for n in range(3))
    right = jnp.concatenate([h, m, h, l, m, h], axis=0)
    change = lax.dot_general(left, right, FIRST, preferred_element_type=F32)[lo:]
    lane = lax.broadcasted_iota(jnp.int32, (P_SIZE - lo, P_SIZE), 1) - r0
    old = jnp.where((lane >= 0) & (lane < b), 0.0, work[lo:, :P_SIZE])
    work[lo:, :P_SIZE] = old - change[:, :P_SIZE]
    work[lo:, P_SIZE:] -= change[:, P_SIZE:]


def kernel(
    shape,
    state_hbm, cen_hbm, half_hbm, rad_hbm, order_hbm, var_hbm,
    out,
    ints, var,
    e_all, foot, tap, tapers, col_c, col_r, var_b, root_b, work, inv, solved, wts, p1, p1_b,
    part, rs, ag, ag_b, cpart, crs, cag, sizes, sizes_b,
    in_s, e_s, x_s,
):
    n_slab, n_mem, n_sub = shape
    n = n_slab * n_sub
    total = n * n_mem
    own, rows = state_hbm.shape

    mi = lax.axis_index("mem")
    slab, sub = lax.axis_index("slab"), lax.axis_index("sub")
    me = slab * n_sub + sub

    def peer(red, mem):
        return {"slab": lax.div(red, n_sub), "sub": lax.rem(red, n_sub), "mem": mem}

    def peer_of(off):
        red = lax.rem(me + lax.rem(off, n), n)
        mem = lax.rem(mi + lax.div(off, n), n_mem)
        return red, mem

    def remote(src, dst, send, recv, device):
        return pltpu.make_async_remote_copy(
            src_ref=src, dst_ref=dst, send_sem=send, recv_sem=recv,
            device_id=device, device_id_type=pl.DeviceIdType.MESH,
        )

    def wait_sent(ref, sem):
        remote(ref, ref, sem, sem, peer(me, mi)).wait_send()

    def wait_recv(ref, sem):
        remote(ref, ref, sem, sem, peer(me, mi)).wait_recv()

    small = [
        pltpu.make_async_copy(a, ints.at[i], in_s.at[0])
        for i, a in enumerate((cen_hbm, half_hbm, rad_hbm, order_hbm))
    ]
    var_copy = pltpu.make_async_copy(var_hbm, var, in_s.at[1])
    state_copy = pltpu.make_async_copy(state_hbm, e_all.at[mi], in_s.at[2])
    for copy in small:
        copy.start()
    var_copy.start()
    state_copy.start()

    barrier = pltpu.get_barrier_semaphore()

    owners = per = part.shape[1]
    middle = (n - per) // 2
    is_owner = jnp.logical_and(me >= middle, me < middle + per)
    is_other = jnp.logical_not(is_owner)

    def greet(to):
        pl.semaphore_signal(barrier, inc=1, device_id=to, device_id_type=pl.DeviceIdType.MESH)

    @pl.when(is_owner)
    def _():
        each(1, total, lambda off: greet(peer(*peer_of(off))))

    @pl.when(is_other)
    def _():
        each(
            0, per * n_mem,
            lambda o: greet(peer(middle + lax.rem(o, per), lax.rem(mi + lax.div(o, per), n_mem))),
        )
        each(1, n_mem, lambda off: greet({"mem": lax.rem(mi + off, n_mem)}))
        each(1, n_sub, lambda off: greet({"sub": lax.rem(sub + off, n_sub)}))

    pltpu.make_async_copy(ints, ints, in_s.at[0]).wait()
    var_copy.wait()

    n_obs = BATCHES * P_SIZE
    picked = jnp.broadcast_to(ints[3].astype(F32), (P_SIZE, n_obs)).T.astype(jnp.int32)
    lane = lax.broadcasted_iota(jnp.int32, (n_obs, P_SIZE), 1)
    masks = [picked == lane + h * P_SIZE for h in range(BATCHES)]

    def pick(ref):
        value = ref[...].astype(F32)
        chosen = 0.0
        for h in range(BATCHES):
            chosen = chosen + jnp.where(masks[h], value[:, h * P_SIZE : (h + 1) * P_SIZE], 0.0)
        return jnp.sum(chosen, axis=1, keepdims=True)

    center = pick(ints.at[0]) - (me * rows).astype(F32)
    width = pick(ints.at[1])
    variance = pick(var)
    col_c[...] = jnp.broadcast_to(center, (n_obs, P_SIZE))
    col_r[...] = jnp.broadcast_to(1.0 / pick(ints.at[2]), (n_obs, P_SIZE))
    var_b[...] = jnp.broadcast_to(variance, (n_obs, P_SIZE))
    root_b[...] = jnp.broadcast_to(jnp.sqrt(variance), (n_obs, P_SIZE))
    steep = -2.0 / (width * width)
    height = 1.0 / jnp.sqrt(width)

    size = rows // TILES

    def tile(c):
        return pl.ds(c * size, size)

    def e_copy(off, c):
        return remote(
            state_hbm.at[:, tile(c)], e_all.at[mi, :, tile(c)], e_s.at[0], e_s.at[1 + c],
            peer(me, lax.rem(mi + off, n_mem)),
        )

    def send_state(c):
        each(1, n_mem, lambda off: e_copy(off, c).start())

    def wait_state(c):
        wait_recv(e_all.at[pl.ds(0, n_mem - 1), :, tile(c)], e_s.at[1 + c])

    def project(b):
        lo = b * P_SIZE

        def foot_tile(t, carry):
            at = pl.multiple_of(t * 256, 256)
            row = lax.broadcasted_iota(jnp.int32, (P_SIZE, 256), 1) + at
            distance = row.astype(F32) - center[lo : lo + P_SIZE]
            shape_f = jnp.exp(distance * distance * steep[lo : lo + P_SIZE]) - FLOOR
            shape_f = jnp.maximum(shape_f, 0.0) * height[lo : lo + P_SIZE]
            foot[lo : lo + P_SIZE, pl.ds(at, 256)] = shape_f.astype(BF16)
            return carry

        lax.fori_loop(0, rows // 256, foot_tile, 0)
        if b == 0:
            state_copy.wait()
        sums = lax.dot_general(
            foot[lo : lo + P_SIZE, :], e_all[mi], LAST, preferred_element_type=F32
        )
        part[b] = sums.reshape(part.shape[1:])

    class Sum:
        def __init__(self, size, index, device, source, target, result, blocks, sem, base, span, high=None):
            self.size, self.index, self.device = size, index, device
            everyone = blocks is not None
            self.source, self.target, self.result, self.blocks = source, target, result, blocks
            self.everyone = everyone
            self.sems, self.base, self.span, self.high = sem, base, span, high
            self.owners = source.shape[0]
            self.relayed = everyone
            self.mine = lax.rem(me + n * per - middle, per) + (0 if everyone else mi * per)
            self.sends = (n_slab * n_mem if everyone else total) - 1
            self.direct = n_mem * per // n_sub
            self.handed = (n_sub - 1) * self.direct

        def owner_of(self, o):
            return self.device(lax.div(o, per) * n + middle + lax.rem(o, per))

        def sem(self, k):
            return self.sems.at[self.base + k]

        def if_owner(self, body, owner=True):
            pl.when(is_owner if owner else is_other)(body)

        def out_copy(self, off):
            o = lax.rem(self.mine + off, self.owners)
            return remote(
                self.source.at[o], self.target.at[self.index],
                self.sem(0), self.sem(1), self.owner_of(o),
            )

        def start(self):
            each(1, self.owners, lambda off: self.out_copy(off).start())
            self.if_owner(lambda: self.out_copy(0).start(), False)

        def start_side(self, q, last):
            def copy(off):
                o = q * per + lax.rem(me + n * per - middle + off, per)
                return remote(
                    self.source.at[o], self.target.at[self.index],
                    self.sem(0), self.sem(1), self.owner_of(o),
                )

            each(1 if last else 0, per, lambda off: copy(off).start())
            if last:
                self.if_owner(lambda: copy(0).start(), False)

        def gather_copy(self, off):
            block = self.result(mi, self.mine)
            to = peer(*peer_of(off))
            if self.relayed:
                to = {
                    "slab": lax.rem(slab + lax.rem(off, n_slab), n_slab),
                    "mem": lax.rem(mi + lax.div(off, n_slab), n_mem),
                }
            return remote(block, block, self.sem(2), self.sem(3), to)

        def relay_copy(self, off):
            blocks = self.blocks.at[:, sub]
            to = {"sub": lax.rem(sub + off, n_sub)}
            return remote(blocks, blocks, self.sem(4), self.sem(5), to)

        def relay(self):
            if self.relayed:
                self.arrived(self.span, self.direct, 3)
                each(1, n_sub, lambda off: self.relay_copy(off).start())

        def high_copy(self, off):
            block = self.high.at[self.mine]
            to = self.device(lax.rem(self.index + off, self.size))
            return remote(block, block, self.sem(6), self.sem(7), to)

        def finish(self):
            def body():
                wait_recv(self.target.at[pl.ds(0, self.size - 1)], self.sem(1))
                block = self.result(mi, self.mine)
                if self.size <= 16:
                    value = self.source[self.mine]
                    for off in range(1, self.size):
                        value = value + self.target[lax.rem(self.index + off, self.size)]
                    block[...] = value
                else:
                    block[...] = self.source[self.mine]

                    def add(off):
                        block[...] += self.target[lax.rem(self.index + off, self.size)]

                    each(1, self.size, add)
                if self.high is not None:
                    self.high[self.mine] = block[...].astype(BF16)
                    each(1, self.size, lambda off: self.high_copy(off).start())
                turn = (lambda off: off) if self.relayed else (lambda off: total - off)
                each(1, self.sends + 1, lambda off: self.gather_copy(turn(off)).start())

            self.if_owner(body)

        def arrived(self, flat, count, sem):
            self.if_owner(lambda: wait_recv(flat.at[pl.ds(0, count - 1)], self.sem(sem)))
            self.if_owner(lambda: wait_recv(flat.at[pl.ds(0, count)], self.sem(sem)), False)

        def gather(self):
            if self.relayed:
                wait_recv(self.span.at[pl.ds(0, self.handed)], self.sem(5))
            else:
                self.arrived(self.span, self.owners, 3)

        def gather_high(self):
            self.arrived(self.high, self.owners, 7)

        def sent(self):
            self.if_owner(
                lambda: wait_sent(self.source.at[pl.ds(0, self.owners - 1)], self.sem(0))
            )
            self.if_owner(lambda: wait_sent(self.source, self.sem(0)), False)
            self.if_owner(lambda: wait_sent(self.span.at[pl.ds(0, self.sends)], self.sem(2)))
            if self.relayed:
                wait_sent(self.span.at[pl.ds(0, self.handed)], self.sem(4))
            if self.high is not None:
                self.if_owner(
                    lambda: wait_sent(sizes_b.at[pl.ds(0, self.size - 1)], self.sem(6))
                )

    projections = [
        Sum(
            n, me, lambda i: peer(i, mi), part.at[b], rs.at[b],
            lambda mem, o, b=b: ag.at[b, lax.div(mem * owners + o, n_sub), lax.rem(mem * owners + o, n_sub)],
            ag.at[b], x_s, 8 * b, sizes, ag_b if b == 0 else None,
        )
        for b in range(BATCHES)
    ]
    changes = Sum(
        total, mi * n + me, lambda i: peer(lax.rem(i, n), lax.div(i, n)), cpart, crs,
        lambda mem, o: cag.at[o], None, x_s, 14, crs,
    )
    project(0)
    pl.when(is_owner)(lambda: pl.semaphore_wait(barrier, total - 1))
    pl.when(is_other)(lambda: pl.semaphore_wait(barrier, per * n_mem + n_mem + n_sub - 2))
    projections[0].start()
    send_state(0)
    send_state(1)
    project(1)

    def taper(b, at):
        lo = b * P_SIZE
        row = lax.broadcasted_iota(jnp.int32, (P_SIZE, size), 1) + at.start
        c = jnp.concatenate([col_c[lo : lo + P_SIZE, :]] * (size // P_SIZE), axis=1)
        r = jnp.concatenate([col_r[lo : lo + P_SIZE, :]] * (size // P_SIZE), axis=1)
        near = jnp.maximum(1.0 - jnp.abs(row.astype(F32) - c) * r, 0.0)
        return near * near * (1.0 / (M - 1))

    for b in range(BATCHES):
        for c in range(TILES):
            tapers[b, :, tile(c)] = taper(b, tile(c))

    projections[1].start()
    projections[0].finish()
    pl.when(is_other)(lambda: send_state(2))

    def slot(b, s):
        step = owners // n_sub
        return ag[b, s * step : (s + 1) * step].reshape(P_SIZE, own)

    def load_work(columns, extra, b):
        h, m, l = (jnp.concatenate(x, axis=1) for x in zip(*(split3(x) for x in columns)))
        cov = lax.dot_general(
            jnp.concatenate([h, h, m, h, m, l], axis=1),
            jnp.concatenate([h, m, h, l, m, h], axis=1),
            LAST, preferred_element_type=F32,
        )
        r = lax.broadcasted_iota(jnp.int32, (P_SIZE, P_SIZE), 0)
        eye = r == lax.broadcasted_iota(jnp.int32, (P_SIZE, P_SIZE), 1)
        v = var_b[b * P_SIZE : (b + 1) * P_SIZE, :]
        work[:, :P_SIZE] = cov * (1.0 / (M - 1)) + jnp.where(eye, v, 0.0)
        lo = P_SIZE
        for x in extra:
            work[:, lo : lo + own] = x
            lo += own

    projections[1].finish()
    projections[0].gather_high()

    side, step = P_SIZE // n_mem, per // n_mem
    for k in range(1, n_mem + 1):
        q = lax.rem(mi + k, n_mem)
        at = pl.ds(pl.multiple_of(q * side, side), side)
        left = ag_b[pl.ds(q * step, step)].reshape(side, own)
        change = 0.0
        for c in range(TILES):
            product = jnp.dot(left, e_all[mi, :, tile(c)], preferred_element_type=F32)
            product = tapers[0, at, tile(c)] * product
            high = product.astype(BF16)
            low = (product - high.astype(F32)).astype(BF16)
            change = change + lax.dot_general(
                jnp.concatenate([high, low], axis=0), foot[P_SIZE : 2 * P_SIZE, tile(c)],
                LAST, preferred_element_type=F32,
            )
        change = change[:side] + change[side:]
        cpart[pl.ds(q * per, per)] = change.reshape(per, cpart.shape[1], P_SIZE)
        changes.start_side(q, k == n_mem)
    pl.when(is_owner)(lambda: send_state(2))
    pl.when(is_other)(lambda: send_state(3))

    projections[0].relay()
    projections[0].gather()
    first = [slot(0, s) for s in range(n_mem)]
    load_work(first, first, 0)
    root_0 = root_b.at[pl.ds(0, P_SIZE)]
    blocks = P_SIZE // BLOCK
    for k in range(blocks // 2):
        block(work, inv, solved, root_0, k)
        if k == 0:
            pl.when(is_owner)(lambda: send_state(3))
    changes.finish()
    for k in range(blocks // 2, blocks):
        block(work, inv, solved, root_0, k)

    def weights(count):
        h, m, l = split3(solved[:, :count])
        left = jnp.concatenate([h, h, m, h, m, l], axis=0)
        h, m, l = split3(inv[...])
        right = jnp.concatenate([h, m, h, l, m, h], axis=0)
        return lax.dot_general(left, right, FIRST, preferred_element_type=F32).astype(BF16)

    wts[...] = weights(M)
    projections[1].relay()
    first_b = [slot(0, s).astype(BF16) for s in range(n_mem)]

    def cross(b, left, at):
        product = 0.0
        for s in range(n_mem):
            product = product + jnp.dot(left[s], e_all[s, :, at], preferred_element_type=F32)
        tap[:, at] = (tapers[b, :, at] * product).astype(BF16)

    def update(at):
        cross(0, first_b, at)
        for s in range(n_mem):
            moved = jnp.dot(
                wts[s * own : (s + 1) * own, :], tap[:, at], preferred_element_type=F32
            )
            e_all[s, :, at] = (e_all[s, :, at].astype(F32) - moved).astype(BF16)

    for c in range(TILES):
        wait_state(c)
        update(tile(c))

    projections[1].gather()
    changes.gather()
    c_full = jnp.concatenate(split3(cag[...].reshape(P_SIZE, P_SIZE).T), axis=0)
    moved = lax.dot_general(c_full, wts[...], LAST, preferred_element_type=F32)
    moved = moved[:P_SIZE] + (moved[P_SIZE : 2 * P_SIZE] + moved[2 * P_SIZE :])
    second = []
    for s in range(n_mem):
        value = slot(1, s) - moved[:, s * own : (s + 1) * own]
        p1[s] = value
        p1_b[s] = value.astype(BF16)
        second.append(value)

    alone = own % P_SIZE == 0
    load_work(second, [p1[mi]] if alone else second, 1)

    used = P_SIZE + (own if alone else M)
    for k in range(blocks):
        block(
            work.at[:, pl.ds(0, used)], inv, solved, root_b.at[pl.ds(P_SIZE, P_SIZE)], k
        )
        cross(1, p1_b, tile(k))
    if alone:
        own_w = weights(own)
    else:
        wts[...] = weights(M)
        own_w = wts[pl.ds(pl.multiple_of(mi * own, own), own), :]

    moved = jnp.dot(own_w, tap[...], preferred_element_type=F32)
    out[...] = (e_all[mi].astype(F32) - moved).astype(BF16)

    wait_sent(e_all.at[pl.ds(0, n_mem - 1)], e_s.at[0])
    for x in projections + [changes]:
        x.sent()


def on_device(shape, state, centers, half_width, radius, order, obs_var):
    n_slab, n_mem, n_sub = shape
    own, rows = state.shape
    n = n_slab * n_sub
    total = n * n_mem
    owners = min(n, 4)
    chunk = P_SIZE // owners
    c_owners = owners * n_mem
    c_chunk = P_SIZE // c_owners
    n_obs = BATCHES * P_SIZE
    operands = (state,) + tuple(
        x[None, :] for x in (centers, half_width, radius, order, obs_var)
    )
    hbm = pl.BlockSpec(memory_space=pltpu.HBM)
    vmem = pl.BlockSpec(memory_space=pltpu.VMEM)
    return pl.pallas_call(
        functools.partial(kernel, shape),
        out_shape=pltpu.VMEM((own, rows), BF16),
        in_specs=[hbm] * 6,
        out_specs=vmem,
        scratch_shapes=[
            pltpu.VMEM((4, 1, n_obs), jnp.int32),
            pltpu.VMEM((1, n_obs), F32),
            pltpu.VMEM((n_mem, own, rows), BF16),
            pltpu.VMEM((n_obs, rows), BF16),
            pltpu.VMEM((P_SIZE, rows), BF16),
            pltpu.VMEM((BATCHES, P_SIZE, rows), F32),
            pltpu.VMEM((n_obs, P_SIZE), F32),
            pltpu.VMEM((n_obs, P_SIZE), F32),
            pltpu.VMEM((n_obs, P_SIZE), F32),
            pltpu.VMEM((n_obs, P_SIZE), F32),
            pltpu.VMEM((P_SIZE, P_SIZE + M), F32),
            pltpu.VMEM((P_SIZE, P_SIZE), F32),
            pltpu.VMEM((P_SIZE, M), F32),
            pltpu.VMEM((M, P_SIZE), BF16),
            pltpu.VMEM((n_mem, P_SIZE, own), F32),
            pltpu.VMEM((n_mem, P_SIZE, own), BF16),
            pltpu.VMEM((BATCHES, owners, chunk, own), F32),
            pltpu.VMEM((BATCHES, n, chunk, own), F32),
            pltpu.VMEM((BATCHES, n_mem * owners // n_sub, n_sub, chunk, own), F32),
            pltpu.VMEM((owners, chunk, own), BF16),
            pltpu.VMEM((c_owners, c_chunk, P_SIZE), F32),
            pltpu.VMEM((total, c_chunk, P_SIZE), F32),
            pltpu.VMEM((c_owners, c_chunk, P_SIZE), F32),
            pltpu.VMEM((total, chunk, own), F32),
            pltpu.VMEM((n, chunk, own), BF16),
            pltpu.SemaphoreType.DMA((3,)),
            pltpu.SemaphoreType.DMA((1 + TILES,)),
            pltpu.SemaphoreType.DMA((18,)),
        ],
        compiler_params=pltpu.CompilerParams(
            collective_id=0, has_side_effects=True, vmem_limit_bytes=40 * 1024 * 1024
        ),
    )(*(pltpu.with_memory_space_constraint(x, pltpu.HBM) for x in operands))


def solution(mesh):
    shape = (mesh.shape["slab"], mesh.shape["mem"], mesh.shape["sub"])
    placed = (P("mem", ("grp", "slab", "sub")), P("grp"), P("grp"), P("grp"), P("grp"), P("grp"))
    return jax.shard_map(
        functools.partial(on_device, shape),
        mesh=mesh,
        in_specs=placed,
        out_specs=P("mem", ("grp", "slab", "sub")),
        check_vma=False,
    )
```
